256 devices in a mesh: row: 8 (over y_hi, x), col: 32 (over z, y_lo, core).
Axes of the slice: x: 4, y: 4 (y_hi: 2, y_lo: 2; y = y_hi * 2 + y_lo), z: 8, core: 2. Of those that a mesh axis runs over, the one named last changes fastest.
Arguments:
- samples: float32 [384, 16384], P(None, ('row', 'col')), may hold values from -6 to 6
- omega: float32 [16384, 16384], P('row', 'col'), may hold values from -0.5 to 3, as said below
Outputs:
- precision: float32 [16384, 16384], P('row', 'col')
The draws below stay inside these ranges and needn't reach their ends.
Inputs may be any that keep to these rules, and one draw needn't show every extreme that they name: omega is symmetric; its diagonal entries lie between 1 and 3, its other entries are much smaller.
All inputs are finite; a program needn't handle non-finite values.
Results may differ from the reference program's by a relative error of at most 0.0003.
Values sent between devices are 32-bit elements; how exact they have to be, the bound alone decides.
A program may use at most 128 MiB of HBM per device.

```python
import jax
import jax.numpy as jnp
from jax import lax

P_SIZE = 16384
SAMPLES = 384
ITERS = 2


def draw_omega(key, part):
    first, second = jax.random.split(jax.random.fold_in(key, 11))
    base = jnp.clip(jax.random.normal(first, (P_SIZE, P_SIZE), jnp.float32), -6.0, 6.0)
    sym = (base + base.T) * 0.5 ** 0.5 * P_SIZE ** (-0.5)
    diagonal = jnp.exp(jax.random.uniform(second, (P_SIZE,), jnp.float32, 0.0, jnp.log(3.0)))
    index = jnp.arange(P_SIZE, dtype=jnp.int32)
    return sym.at[index, index].set(diagonal)


def shard_levels(key, extent, pieces, smallest, top_value):
    def one(axis_at, parts):
        draws = jax.random.uniform(jax.random.fold_in(jax.random.fold_in(key, 6), axis_at), (parts,), jnp.float32, smallest / len(pieces), top_value / len(pieces))
        return jnp.repeat(jnp.exp(draws), extent[axis_at] // parts).reshape((-1,) + (1,) * (len(extent) - axis_at - 1))

    level = one(*pieces[0])
    for cut in pieces[1:]:
        level = level * one(*cut)
    return level


def gaussian(rng, shape, width, bound, pieces=(), kind=jnp.bfloat16):
    drawn = width * jax.random.normal(rng, shape, jnp.float32)
    if pieces:
        drawn = drawn * shard_levels(rng, shape, pieces, -0.22, 0.18)
    return jnp.clip(drawn, -bound, bound).astype(kind)


def setup_inputs(seed: int = 0) -> dict:
    splits = jax.random.split(jax.random.key(seed), 3)
    samples = gaussian(splits[0], (SAMPLES, P_SIZE), 1.0, 6.0, ((1, 256),), jnp.float32)
    omega = draw_omega(jax.random.fold_in(splits[2], 71), 0)
    return dict(samples=samples, omega=omega)


step_size = 0.01
penalty = 0.25


def reference(samples, omega):
    precision = omega
    index = jnp.arange(P_SIZE, dtype=jnp.int32)
    for turn in range(ITERS):
        projected = jnp.dot(samples, precision, precision=lax.Precision.HIGHEST)
        cross = lax.dot_general(samples, projected, (((0,), (0,)), ((), ())), precision=lax.Precision.HIGHEST) / SAMPLES
        gradient = 0.5 * (cross + cross.T)
        diagonal = jnp.diagonal(precision)
        moved = precision - step_size * gradient
        shrunk = jnp.sign(moved) * jnp.maximum(jnp.abs(moved) - step_size * penalty, 0.0)
        new_diag = diagonal - step_size * (jnp.diagonal(gradient) - 1.0 / diagonal)
        precision = shrunk.at[index, index].set(new_diag)
    return precision
```

```python
import functools

import jax
import jax.numpy as jnp
from jax import lax
from jax.experimental import pallas as pl
from jax.experimental.pallas import tpu as pltpu
from jax.sharding import PartitionSpec as P

ITERS = 2
STEP = 0.01
PENALTY = 0.25
S = 384
EARLY = 128
MESH = pl.DeviceIdType.MESH
F32 = jnp.float32
BF16 = jnp.bfloat16
VMEM_LIMIT = 56 * 2**20


def place():
    r = lax.axis_index("row")
    c = lax.axis_index("col")
    return r % 4, (r // 4) * 2 + (c // 2) % 2, c // 4, c % 2


def device(x, y, z, k):
    return (y // 2) * 4 + x, z * 4 + (y % 2) * 2 + k


def rows(start, size):
    return pl.ds(pl.multiple_of(start, 64), size)


class Copies:
    def __init__(self, send, recv):
        self.send, self.recv = send, recv
        self.pending = []

    def make(self, slot, src, dst, to):
        return pltpu.make_async_remote_copy(
            src_ref=src, dst_ref=dst, send_sem=self.send.at[slot], recv_sem=self.recv.at[slot],
            device_id=to, device_id_type=MESH)

    def start(self, slot, src, dst, to):
        copy = self.make(slot, src, dst, to)
        copy.start()
        self.pending.append((copy, None))
        return copy

    def start_if(self, cond, slot, src, dst, to, send=None):
        copy = pltpu.make_async_remote_copy(
            src_ref=src, dst_ref=dst, send_sem=self.send.at[slot if send is None else send],
            recv_sem=self.recv.at[slot], device_id=to, device_id_type=MESH)

        @pl.when(cond)
        def _():
            copy.start()

        self.pending.append((copy, cond))

    def finish(self):
        for copy, cond in self.pending:
            if cond is None:
                copy.wait_send()
            else:
                @pl.when(cond)
                def _():
                    copy.wait_send()


def greet(partners):
    barrier = pltpu.get_barrier_semaphore()
    for partner in partners:
        pl.semaphore_signal(barrier, inc=1, device_id=partner, device_id_type=MESH)
    pl.semaphore_wait(barrier, len(partners))


def column_piece(buf, x, y, d, e=0):
    return buf.at[rows((((y + e) % 4) // 2 * 4 + (x + 4 - d) % 4) * 64, 64)]


AROUND = (1, 3, 2)


def column_start(cp, buf, x, y, z, k, base):
    mine = column_piece(buf, x, y, 0)
    for d in AROUND:
        cp.start(base + d, mine, mine, device((x + d) % 4, y, z, k))
    cp.start(base, mine, mine, device(x, (y + 2) % 4, z, k))


def column_middle(cp, buf, x, y, z, k, base):
    theirs = column_piece(buf, x, y, 0, 2)
    cp.make(base, theirs, theirs, (0, 0)).wait_recv()
    for d in AROUND:
        cp.start(base + 3 + d, theirs, theirs, device((x + d) % 4, y, z, k))


def column_end(cp, buf, x, y, z, k, base):
    mine = column_piece(buf, x, y, 0)
    for d in AROUND:
        cp.make(base + d, mine, mine, (0, 0)).wait_recv()
        cp.make(base + 3 + d, mine, mine, (0, 0)).wait_recv()


def gather_samples_kernel(own_ref, panel, block, send, recv, sem):
    x, y, z, k = place()
    yl, yh = y % 2, y // 2
    r, c = yh * 4 + x, z * 4 + yl * 2 + k
    up = device(x, y, (z + 1) % 8, k)
    down = device(x, y, (z + 7) % 8, k)
    lo = device(x, yh * 2 + 1 - yl, z, k)
    core = device(x, y, z, 1 - k)
    to_r, to_c = c % 8, r * 4 + c // 8
    own_b = c * 8 + r
    from_r, from_c = own_b // 32, own_b % 32
    moves = (to_r * 32 + to_c) != (r * 32 + c)
    group = [device((x + d) % 4, (y + e) % 4, z, k) for d in range(4) for e in (0, 2) if d or e]
    cp = Copies(send, recv)

    barrier = pltpu.get_barrier_semaphore()
    partners = [up, down, lo, core] + group
    for partner in partners:
        pl.semaphore_signal(barrier, inc=1, device_id=partner, device_id_type=MESH)

    @pl.when(moves)
    def _():
        pl.semaphore_signal(barrier, inc=1, device_id=(from_r, from_c), device_id_type=MESH)

    def at(zz, l):
        return panel.at[rows((zz * 4 + l * 2 + k) * 64, 64)]

    def early(ref):
        return ref.at[:, pl.ds(0, EARLY)]

    def late(ref):
        return ref.at[:, pl.ds(EARLY, S - EARLY)]

    panel[rows(c * 64, 64)] = own_ref[...]
    pl.semaphore_wait(barrier, len(partners) + jnp.where(moves, 1, 0))

    own = at(z, yl)
    E_OWN, UP, DOWN, UP_E, DOWN_E, LO, CORE, CORE_LO, COL = 0, 1, 5, 8, 12, 16, 24, 32, 40
    PERM = 47
    cp.start(E_OWN, early(own), early(own), lo)
    cp.start(UP, own, own, up)
    cp.start(DOWN, own, own, down)
    cp.start_if(moves, PERM, own, block.at[rows(to_r * 64, 64)], (to_r, to_c))

    @pl.when(jnp.logical_not(moves))
    def _():
        block[rows(r * 64, 64)] = own_ref[...]

    cp.start(LO, late(own), late(own), lo)
    cp.start(CORE, own, own, core)
    cp.make(E_OWN, early(own), early(own), lo).wait_recv()
    e = early(at(z, 1 - yl))
    cp.start(UP_E, e, e, up)
    cp.start(DOWN_E, e, e, down)

    def lo_arrived(i, zz):
        piece = at(zz, 1 - yl)
        cp.make(LO + i, late(piece), late(piece), lo).wait_recv()
        cp.start(CORE_LO + i, piece, piece, core)

    n = 1
    for t in range(1, 5):
        a = at((z + 8 - t) % 8, yl)
        b = at((z + t) % 8, yl)
        cp.make(UP + t - 1, a, a, up).wait_recv()
        if t < 4:
            cp.start(UP + t, a, a, up)
            cp.make(DOWN + t - 1, b, b, down).wait_recv()
            if t < 3:
                cp.start(DOWN + t, b, b, down)
        ea = early(at((z + 8 - t) % 8, 1 - yl))
        eb = early(at((z + t) % 8, 1 - yl))
        if t < 4:
            cp.make(UP_E + t - 1, ea, ea, up).wait_recv()
            if t < 3:
                cp.start(UP_E + t, ea, ea, up)
        cp.make(DOWN_E + t - 1, eb, eb, down).wait_recv()
        if t < 4:
            cp.start(DOWN_E + t, eb, eb, down)
        cp.start(LO + 2 * t - 1, late(a), late(a), lo)
        cp.start(CORE + 2 * t - 1, a, a, core)
        if t < 4:
            cp.start(LO + 2 * t, late(b), late(b), lo)
            cp.start(CORE + 2 * t, b, b, core)
        if t == 2:
            @pl.when(moves)
            def _():
                cp.make(PERM, own, own, lo).wait_recv()

            column_start(cp, block, x, y, z, k, COL)
        if t == 3:
            column_middle(cp, block, x, y, z, k, COL)
        if t == 1:
            lo_arrived(0, z)
        else:
            lo_arrived(2 * t - 3, (z + 8 - (t - 1)) % 8)
            lo_arrived(2 * t - 2, (z + t - 1) % 8)
    lo_arrived(7, (z + 4) % 8)
    column_end(cp, block, x, y, z, k, COL)
    for i in range(8):
        cp.make(CORE + i, own, own, core).wait_recv()
        cp.make(CORE_LO + i, own, own, core).wait_recv()
    cp.finish()


HALVES = 2
CHUNK = 64 // HALVES
CHUNKS = 4 * HALVES


def gather_projected_kernel(part, panel_out, block, panel, inbox, send, recv, sem):
    x, y, z, k = place()
    yl, yh = y % 2, y // 2
    r = yh * 4 + x
    up = device(x, y, (z + 1) % 8, k)
    down = device(x, y, (z + 7) % 8, k)
    lo = device(x, yh * 2 + 1 - yl, z, k)
    far = device(x, 3 - y, z, k)
    core = device(x, y, z, 1 - k)
    group = [((x + d) % 4, (y + e) % 4) for d in (2, 1, 3, 0) for e in (2, 0) if d or e]
    cp = Copies(send, recv)
    greet([up, down, lo, far, core] + [device(tx, ty, z, k) for tx, ty in group])

    for i, (tx, ty) in enumerate(group):
        tr = (ty // 2) * 4 + tx
        cp.start(i, part.at[rows(tr * 64, 64)], inbox.at[i], device(tx, ty, z, k))
    total = part[rows(r * 64, 64)]
    for i in range(7):
        cp.make(i, inbox.at[i], inbox.at[i], core).wait_recv()
        total = total + inbox[i]
    block[rows(r * 64, 64)] = total
    COL = 7
    column_start(cp, block, x, y, z, k, COL)

    lane = (yl * 2 + k) * 512
    flane = ((1 - yl) * 2 + k) * 512
    fyh = 1 - yh

    def within(h, q):
        d = (0,) + AROUND
        return h * 256 + (x + 4 - d[q // HALVES]) % 4 * 64 + q % HALVES * CHUNK

    def full(base, h, q):
        return panel.at[pl.ds(pl.multiple_of(base + within(h, q), CHUNK), CHUNK)]

    def early(ref):
        return ref.at[:, pl.ds(0, EARLY)]

    def late(ref):
        return ref.at[:, pl.ds(EARLY, S - EARLY)]

    d0 = (z + 8 - x) % 8
    near = jnp.where(jnp.logical_or(d0 <= 2, d0 >= 6), 0, 1)
    other = 1 - near
    Z = 14
    ZD = Z + 4 * CHUNKS
    FAR = ZD + 4 * CHUNKS
    LO = FAR + 2 * CHUNKS
    LOF = LO + CHUNKS
    CORE = LOF + CHUNKS

    def relay(s, q):
        d = (d0 + 4 * s) % 8
        mine = s == yh
        base = jnp.where(mine, lane, 2048)
        a, b = full(base, yh, q), early(full(base, fyh, q))
        slot = Z + (s * CHUNKS + q) * 2

        @pl.when(d == 0)
        def _():
            at = pl.ds(pl.multiple_of(within(yh, q), CHUNK), CHUNK)
            to = pl.ds(pl.multiple_of(base + within(yh, q), CHUNK), CHUNK)
            panel[to] = block[at]

        @pl.when(d != 0)
        def _():
            cp.make(slot, a, a, up).wait_recv()

        cp.start_if(d <= 3, slot, a, a, up)
        cp.start_if(jnp.logical_or(d == 0, d >= 6), slot, a, a, down, slot + ZD - Z)
        la, lb = full(lane, yh, q), early(full(lane, fyh, q))
        theirs = jnp.logical_not(mine)
        cp.start_if(theirs, FAR + 2 * q, a, la, far)
        cp.start_if(mine, LO + q, late(la), late(la), lo)
        cp.start_if(mine, CORE + q, la, la, core)

        @pl.when(d == 0)
        def _():
            at = pl.ds(pl.multiple_of(within(fyh, q), CHUNK), CHUNK)
            to = pl.ds(pl.multiple_of(base + within(fyh, q), CHUNK), CHUNK)
            panel[to, :EARLY] = block[at, :EARLY]

        @pl.when(d != 0)
        def _():
            cp.make(slot + 1, b, b, up).wait_recv()

        cp.start_if(d <= 2, slot + 1, b, b, up)
        cp.start_if(jnp.logical_or(d == 0, d >= 5), slot + 1, b, b, down, slot + 1 + ZD - Z)
        cp.start_if(theirs, FAR + 2 * q + 1, b, lb, far)

    def far_in(q):
        a, b = full(flane, fyh, q), early(full(flane, yh, q))
        cp.make(FAR + 2 * q, a, a, far).wait_recv()
        cp.start(LOF + q, late(a), late(a), lo)
        cp.start(CORE + CHUNKS + q, a, a, core)
        cp.make(FAR + 2 * q + 1, b, b, far).wait_recv()

    def lo_in(q):
        a = full(flane, yh, q)
        cp.make(LO + q, late(a), late(a), lo).wait_recv()
        cp.start(CORE + 2 * CHUNKS + q, a, a, core)

    def lof_in(q):
        a = full(lane, fyh, q)
        cp.make(LOF + q, late(a), late(a), lo).wait_recv()
        cp.start(CORE + 3 * CHUNKS + q, a, a, core)

    piece = column_piece(block, x, y, 0)
    column_middle(cp, block, x, y, z, k, COL)
    for q in range(CHUNKS + 4):
        if q < CHUNKS:
            if q % HALVES == 0 and q:
                d = AROUND[q // HALVES - 1]
                cp.make(COL + d, piece, piece, core).wait_recv()
                cp.make(COL + 3 + d, piece, piece, core).wait_recv()
            relay(near, q)
        if 2 <= q < CHUNKS + 2:
            relay(other, q - 2)
        if 3 <= q < CHUNKS + 3:
            far_in(q - 3)
            lo_in(q - 3)
        if 4 <= q < CHUNKS + 4:
            lof_in(q - 4)
    for g in range(4):
        for q in range(CHUNKS):
            ref = full(lane, yh, q)
            cp.make(CORE + g * CHUNKS + q, ref, ref, core).wait_recv()
    cp.finish()
    out = pltpu.make_async_copy(panel.at[pl.ds(0, 2048)], panel_out, sem)
    out.start()
    out.wait()


def split(a):
    hi = a.astype(BF16)
    return hi, (a - hi.astype(F32)).astype(BF16)


def dot3(ah, al, bh, bl, dims):
    d = lambda p, q: lax.dot_general(p, q, (dims, ((), ())), preferred_element_type=F32)
    return d(ah, bh) + (d(ah, bl) + d(al, bh))


TILE = 256
NN = ((1,), (0,))
NT = ((1,), (1,))


def first_partial_kernel(panel, omega, xh_out, xl_out, part, acc):
    i = pl.program_id(0)
    xh, xl = split(panel[...].T)
    xh_out[...] = xh
    xl_out[...] = xl
    oh, ol = split(omega[...])

    @pl.when(i == 0)
    def _():
        acc[...] = jnp.zeros_like(acc)

    acc[...] += dot3(xh, xl, oh, ol, NN)

    @pl.when(i == pl.num_programs(0) - 1)
    def _():
        part[...] = acc[...].T


def update_kernel(last, count, xr, yr, xc, yc, omega, xh, xl, *rest):
    if last:
        out, rh, rl = rest
    else:
        out, part, rh, rl, acc = rest
    i = pl.program_id(0)
    row0 = lax.axis_index("row") * 2048 + i * TILE
    col0 = lax.axis_index("col") * 512

    @pl.when(i == 0)
    def _():
        h, l = split(yc[...])
        rh[:, :S] = h
        rl[:, :S] = l
        h, l = split(xc[...])
        rh[:, S:] = h
        rl[:, S:] = l
        if not last:
            acc[...] = jnp.zeros_like(acc)

    ah, al = split(jnp.concatenate([xr[...], yr[...]], axis=1))
    cross = dot3(ah, al, rh[...], rl[...], NT)
    old = omega[...]
    moved = old - (STEP * 0.5 / count) * cross
    thr = STEP * PENALTY
    new = moved - jnp.clip(moved, -thr, thr)
    out[...] = new

    @pl.when(jnp.logical_and(row0 < col0 + 512, col0 < row0 + TILE))
    def _():
        gr = row0 + lax.broadcasted_iota(jnp.int32, (TILE, 512), 0)
        gc = col0 + lax.broadcasted_iota(jnp.int32, (TILE, 512), 1)
        on = gr == gc
        safe = jnp.where(on, old, 1.0)
        out[...] = jnp.where(on, moved + STEP / safe, new)

    if not last:
        nh, nl = split(out[...])
        acc[...] += dot3(xh[...], xl[...], nh, nl, NN)

        @pl.when(i == pl.num_programs(0) - 1)
        def _():
            part[...] = acc[...].T


def shape(*dims, dtype=F32):
    return jax.ShapeDtypeStruct(dims, dtype)


def vm():
    return pl.BlockSpec(memory_space=pltpu.VMEM)


def gather_samples(own):
    n = 48
    return pl.pallas_call(
        gather_samples_kernel,
        out_shape=(shape(2048, S), shape(512, S)),
        in_specs=[vm()], out_specs=(vm(), vm()),
        scratch_shapes=[pltpu.SemaphoreType.DMA((n,)), pltpu.SemaphoreType.DMA((n,)), pltpu.SemaphoreType.DMA],
        compiler_params=pltpu.CompilerParams(collective_id=0, has_side_effects=True, vmem_limit_bytes=VMEM_LIMIT),
        name="gather_samples",
    )(own)


def gather_projected(part):
    n = 14 + 16 * CHUNKS
    return pl.pallas_call(
        gather_projected_kernel,
        out_shape=(shape(2048, S), shape(512, S)),
        in_specs=[vm()], out_specs=(vm(), vm()),
        scratch_shapes=[pltpu.VMEM((2560, S), F32), pltpu.VMEM((7, 64, S), F32),
                        pltpu.SemaphoreType.DMA((n,)), pltpu.SemaphoreType.DMA((n,)), pltpu.SemaphoreType.DMA],
        compiler_params=pltpu.CompilerParams(collective_id=1, has_side_effects=True, vmem_limit_bytes=VMEM_LIMIT),
        name="gather_projected",
    )(part)


def first_partial(panel, omega):
    return pl.pallas_call(
        first_partial_kernel,
        grid=(2048 // TILE,),
        out_shape=(shape(S, 2048, dtype=BF16), shape(S, 2048, dtype=BF16), shape(512, S)),
        in_specs=[pl.BlockSpec((TILE, S), lambda i: (i, 0)), pl.BlockSpec((TILE, 512), lambda i: (i, 0))],
        out_specs=(pl.BlockSpec((S, TILE), lambda i: (0, i)), pl.BlockSpec((S, TILE), lambda i: (0, i)),
                   pl.BlockSpec((512, S), lambda i: (0, 0))),
        scratch_shapes=[pltpu.VMEM((S, 512), F32)],
        compiler_params=pltpu.CompilerParams(vmem_limit_bytes=VMEM_LIMIT),
        name="first_partial",
    )(panel, omega)


def update(last, xr, yr, xc, yc, omega, xh, xl):
    tile = pl.BlockSpec((TILE, S), lambda i: (i, 0))
    whole = pl.BlockSpec((512, S), lambda i: (0, 0))
    square = pl.BlockSpec((TILE, 512), lambda i: (i, 0))
    tall = pl.BlockSpec((S, TILE), lambda i: (0, i))
    scratch = [pltpu.VMEM((512, 2 * S), BF16), pltpu.VMEM((512, 2 * S), BF16)]
    if last:
        out_shape, out_specs = shape(2048, 512), square
    else:
        out_shape, out_specs = (shape(2048, 512), shape(512, S)), (square, whole)
        scratch.append(pltpu.VMEM((S, 512), F32))
    return pl.pallas_call(
        functools.partial(update_kernel, last, S),
        grid=(2048 // TILE,),
        out_shape=out_shape,
        in_specs=[tile, tile, whole, whole, square, tall, tall],
        out_specs=out_specs,
        scratch_shapes=scratch,
        compiler_params=pltpu.CompilerParams(vmem_limit_bytes=VMEM_LIMIT),
        name="update_last" if last else "update",
    )(xr, yr, xc, yc, omega, xh, xl)


def body(samples, omega):
    own = samples.T
    xr, xc = gather_samples(own)
    xh, xl, part = first_partial(xr, omega)
    yr, yc = gather_projected(part)
    omega, part = update(False, xr, yr, xc, yc, omega, xh, xl)
    yr, yc = gather_projected(part)
    return update(True, xr, yr, xc, yc, omega, xh, xl)


def solution(mesh):
    in_specs = (P(None, ("row", "col")), P("row", "col"))
    out_specs = P("row", "col")
    return jax.shard_map(body, mesh=mesh, in_specs=in_specs, out_specs=out_specs, check_vma=False)
```

```python
import functools

import jax
import jax.numpy as jnp
from jax import lax
from jax.experimental import pallas as pl
from jax.experimental.pallas import tpu as pltpu
from jax.sharding import PartitionSpec as P

ITERS = 2
STEP = 0.01
PENALTY = 0.25
S = 384
EARLY = 128
MESH = pl.DeviceIdType.MESH
F32 = jnp.float32
BF16 = jnp.bfloat16
VMEM_LIMIT = 56 * 2**20


def place():
    r = lax.axis_index("row")
    c = lax.axis_index("col")
    return r % 4, (r // 4) * 2 + (c // 2) % 2, c // 4, c % 2


def device(x, y, z, k):
    return (y // 2) * 4 + x, z * 4 + (y % 2) * 2 + k


def rows(start, size):
    return pl.ds(pl.multiple_of(start, 64), size)


class Copies:
    def __init__(self, send, recv):
        self.send, self.recv = send, recv
        self.pending = []

    def make(self, slot, src, dst, to):
        return pltpu.make_async_remote_copy(
            src_ref=src, dst_ref=dst, send_sem=self.send.at[slot], recv_sem=self.recv.at[slot],
            device_id=to, device_id_type=MESH)

    def start(self, slot, src, dst, to):
        copy = self.make(slot, src, dst, to)
        copy.start()
        self.pending.append((copy, None))
        return copy

    def start_if(self, cond, slot, src, dst, to, send=None):
        copy = pltpu.make_async_remote_copy(
            src_ref=src, dst_ref=dst, send_sem=self.send.at[slot if send is None else send],
            recv_sem=self.recv.at[slot], device_id=to, device_id_type=MESH)

        @pl.when(cond)
        def _():
            copy.start()

        self.pending.append((copy, cond))

    def finish(self):
        for copy, cond in self.pending:
            if cond is None:
                copy.wait_send()
            else:
                @pl.when(cond)
                def _():
                    copy.wait_send()


def greet(partners):
    barrier = pltpu.get_barrier_semaphore()
    for partner in partners:
        pl.semaphore_signal(barrier, inc=1, device_id=partner, device_id_type=MESH)
    pl.semaphore_wait(barrier, len(partners))


def column_piece(buf, x, y, d, e=0):
    return buf.at[rows((((y + e) % 4) // 2 * 4 + (x + 4 - d) % 4) * 64, 64)]


AROUND = (1, 3, 2)


def column_start(cp, buf, x, y, z, k, base):
    mine = column_piece(buf, x, y, 0)
    for d in AROUND:
        cp.start(base + d, mine, mine, device((x + d) % 4, y, z, k))
    cp.start(base, mine, mine, device(x, (y + 2) % 4, z, k))


def column_middle(cp, buf, x, y, z, k, base):
    theirs = column_piece(buf, x, y, 0, 2)
    cp.make(base, theirs, theirs, (0, 0)).wait_recv()
    for d in AROUND:
        cp.start(base + 3 + d, theirs, theirs, device((x + d) % 4, y, z, k))


def column_end(cp, buf, x, y, z, k, base):
    mine = column_piece(buf, x, y, 0)
    for d in AROUND:
        cp.make(base + d, mine, mine, (0, 0)).wait_recv()
        cp.make(base + 3 + d, mine, mine, (0, 0)).wait_recv()


def gather_samples_kernel(own_ref, panel, block, send, recv, sem):
    x, y, z, k = place()
    yl, yh = y % 2, y // 2
    r, c = yh * 4 + x, z * 4 + yl * 2 + k
    up = device(x, y, (z + 1) % 8, k)
    down = device(x, y, (z + 7) % 8, k)
    lo = device(x, yh * 2 + 1 - yl, z, k)
    core = device(x, y, z, 1 - k)
    to_r, to_c = c % 8, r * 4 + c // 8
    own_b = c * 8 + r
    from_r, from_c = own_b // 32, own_b % 32
    moves = (to_r * 32 + to_c) != (r * 32 + c)
    group = [device((x + d) % 4, (y + e) % 4, z, k) for d in range(4) for e in (0, 2) if d or e]
    cp = Copies(send, recv)

    barrier = pltpu.get_barrier_semaphore()
    partners = [up, down, lo, core] + group
    for partner in partners:
        pl.semaphore_signal(barrier, inc=1, device_id=partner, device_id_type=MESH)

    @pl.when(moves)
    def _():
        pl.semaphore_signal(barrier, inc=1, device_id=(from_r, from_c), device_id_type=MESH)

    def at(zz, l):
        return panel.at[rows((zz * 4 + l * 2 + k) * 64, 64)]

    def early(ref):
        return ref.at[:, pl.ds(0, EARLY)]

    def late(ref):
        return ref.at[:, pl.ds(EARLY, S - EARLY)]

    panel[rows(c * 64, 64)] = own_ref[...]
    pl.semaphore_wait(barrier, len(partners) + jnp.where(moves, 1, 0))

    own = at(z, yl)
    E_OWN, UP, DOWN, UP_E, DOWN_E, LO, CORE, CORE_LO, COL = 0, 1, 5, 8, 12, 16, 24, 32, 40
    PERM = 47
    cp.start(E_OWN, early(own), early(own), lo)
    cp.start(UP, own, own, up)
    cp.start(DOWN, own, own, down)
    cp.start_if(moves, PERM, own, block.at[rows(to_r * 64, 64)], (to_r, to_c))

    @pl.when(jnp.logical_not(moves))
    def _():
        block[rows(r * 64, 64)] = own_ref[...]

    cp.start(LO, late(own), late(own), lo)
    cp.start(CORE, own, own, core)
    cp.make(E_OWN, early(own), early(own), lo).wait_recv()
    e = early(at(z, 1 - yl))
    cp.start(UP_E, e, e, up)
    cp.start(DOWN_E, e, e, down)

    def lo_arrived(i, zz):
        piece = at(zz, 1 - yl)
        cp.make(LO + i, late(piece), late(piece), lo).wait_recv()
        cp.start(CORE_LO + i, piece, piece, core)

    n = 1
    for t in range(1, 5):
        a = at((z + 8 - t) % 8, yl)
        b = at((z + t) % 8, yl)
        cp.make(UP + t - 1, a, a, up).wait_recv()
        if t < 4:
            cp.start(UP + t, a, a, up)
            cp.make(DOWN + t - 1, b, b, down).wait_recv()
            if t < 3:
                cp.start(DOWN + t, b, b, down)
        ea = early(at((z + 8 - t) % 8, 1 - yl))
        eb = early(at((z + t) % 8, 1 - yl))
        if t < 4:
            cp.make(UP_E + t - 1, ea, ea, up).wait_recv()
            if t < 3:
                cp.start(UP_E + t, ea, ea, up)
        cp.make(DOWN_E + t - 1, eb, eb, down).wait_recv()
        if t < 4:
            cp.start(DOWN_E + t, eb, eb, down)
        cp.start(LO + 2 * t - 1, late(a), late(a), lo)
        cp.start(CORE + 2 * t - 1, a, a, core)
        if t < 4:
            cp.start(LO + 2 * t, late(b), late(b), lo)
            cp.start(CORE + 2 * t, b, b, core)
        if t == 2:
            @pl.when(moves)
            def _():
                cp.make(PERM, own, own, lo).wait_recv()

            column_start(cp, block, x, y, z, k, COL)
        if t == 3:
            column_middle(cp, block, x, y, z, k, COL)
        if t == 1:
            lo_arrived(0, z)
        else:
            lo_arrived(2 * t - 3, (z + 8 - (t - 1)) % 8)
            lo_arrived(2 * t - 2, (z + t - 1) % 8)
    lo_arrived(7, (z + 4) % 8)
    column_end(cp, block, x, y, z, k, COL)
    for i in range(8):
        cp.make(CORE + i, own, own, core).wait_recv()
        cp.make(CORE_LO + i, own, own, core).wait_recv()
    cp.finish()


HALVES = 2
CHUNK = 64 // HALVES
CHUNKS = 4 * HALVES
LAGS = (CHUNKS, CHUNKS // 2, 0)
EARLY_LAG = HALVES
FAR_LAG = EARLY_LAG + 1
LOF_LAG = FAR_LAG + 2


def gather_projected_kernel(part, panel_out, block, panel, inbox, send, recv, sem):
    x, y, z, k = place()
    yl, yh = y % 2, y // 2
    r = yh * 4 + x
    up = device(x, y, (z + 1) % 8, k)
    down = device(x, y, (z + 7) % 8, k)
    lo = device(x, yh * 2 + 1 - yl, z, k)
    far = device(x, 3 - y, z, k)
    core = device(x, y, z, 1 - k)
    group = [((x + d) % 4, (y + e) % 4) for d in (2, 1, 3, 0) for e in (2, 0) if d or e]
    cp = Copies(send, recv)
    greet([up, down, lo, far, core] + [device(tx, ty, z, k) for tx, ty in group])

    for i, (tx, ty) in enumerate(group):
        tr = (ty // 2) * 4 + tx
        cp.start(i, part.at[rows(tr * 64, 64)], inbox.at[i], device(tx, ty, z, k))
    total = part[rows(r * 64, 64)]
    for i in range(7):
        cp.make(i, inbox.at[i], inbox.at[i], core).wait_recv()
        total = total + inbox[i]
    block[rows(r * 64, 64)] = total
    COL = 7
    column_start(cp, block, x, y, z, k, COL)

    lane = (yl * 2 + k) * 512
    flane = ((1 - yl) * 2 + k) * 512
    fyh = 1 - yh

    def within(h, q):
        n = q // HALVES
        d = jnp.where(n == 2, 3, jnp.where(n == 3, 2, n))
        return h * 256 + (x + 4 - d) % 4 * 64 + q % HALVES * CHUNK

    def full(base, h, q):
        return panel.at[pl.ds(pl.multiple_of(base + within(h, q), CHUNK), CHUNK)]

    def early(ref):
        return ref.at[:, pl.ds(0, EARLY)]

    def late(ref):
        return ref.at[:, pl.ds(EARLY, S - EARLY)]

    d0 = (z + 8 - x) % 8
    near = jnp.where(jnp.logical_or(d0 <= 2, d0 >= 6), 0, 1)
    hops = (d0 + 4 * near) % 8
    hops = jnp.where(hops > 4, 8 - hops, hops)
    lag = jnp.where(hops == 0, LAGS[0], jnp.where(hops == 1, LAGS[1], LAGS[2]))
    mine_lag = jnp.where(near == yh, 0, lag)
    Z = 14
    ZD = Z + 4 * CHUNKS
    FAR = ZD + 4 * CHUNKS
    LO = FAR + 2 * CHUNKS
    LOF = LO + CHUNKS
    CORE = LOF + CHUNKS

    def copy(slot, src, dst, to, send_slot=None):
        return pltpu.make_async_remote_copy(
            src_ref=src, dst_ref=dst, send_sem=send.at[slot if send_slot is None else send_slot],
            recv_sem=recv.at[slot], device_id=to, device_id_type=MESH)

    def when(cond, f):
        pl.when(cond)(f)

    def at(base, h, q):
        return pl.ds(pl.multiple_of(base + within(h, q), CHUNK), CHUNK)

    def whole_copies(s, q):
        d = (d0 + 4 * s) % 8
        mine = s == yh
        ref = full(jnp.where(mine, lane, 2048), yh, q)
        to = full(lane, yh, q)
        slot = Z + (s * CHUNKS + q) * 2
        return d, ref, copy(slot, ref, ref, up), [
            (d <= 3, copy(slot, ref, ref, up)),
            (jnp.logical_or(d == 0, d >= 6), copy(slot, ref, ref, down, slot + ZD - Z)),
            (jnp.logical_not(mine), copy(FAR + 2 * q, ref, to, far)),
            (mine, copy(LO + q, late(to), late(to), lo)),
            (mine, copy(CORE + q, to, to, core)),
        ]

    def early_copies(s, q):
        d = (d0 + 4 * s) % 8
        mine = s == yh
        ref = early(full(jnp.where(mine, lane, 2048), fyh, q))
        to = early(full(lane, fyh, q))
        slot = Z + (s * CHUNKS + q) * 2 + 1
        return d, ref, copy(slot, ref, ref, up), [
            (d <= 2, copy(slot, ref, ref, up)),
            (jnp.logical_or(d == 0, d >= 5), copy(slot, ref, ref, down, slot + ZD - Z)),
            (jnp.logical_not(mine), copy(FAR + 2 * q + 1, ref, to, far)),
        ]

    def relay_whole(s, q):
        d, ref, arrival, copies = whole_copies(s, q)

        @pl.when(d == 0)
        def _():
            panel[at(jnp.where(s == yh, lane, 2048), yh, q)] = block[at(0, yh, q)]

        @pl.when(d != 0)
        def _():
            arrival.wait_recv()

        for cond, c in copies:
            when(cond, c.start)

    def relay_early(s, q):
        d, ref, arrival, copies = early_copies(s, q)

        @pl.when(d == 0)
        def _():
            panel[at(jnp.where(s == yh, lane, 2048), fyh, q), :EARLY] = block[at(0, fyh, q), :EARLY]

        @pl.when(d != 0)
        def _():
            arrival.wait_recv()

        for cond, c in copies:
            when(cond, c.start)

    def far_copies(q):
        a, b = full(flane, fyh, q), early(full(flane, yh, q))
        return [copy(FAR + 2 * q, a, a, far), copy(FAR + 2 * q + 1, b, b, far)], [
            copy(LOF + q, late(a), late(a), lo), copy(CORE + CHUNKS + q, a, a, core)]

    def lo_copies(q):
        a = full(flane, yh, q)
        return [copy(LO + q, late(a), late(a), lo)], [copy(CORE + 2 * CHUNKS + q, a, a, core)]

    def lof_copies(q):
        a = full(lane, fyh, q)
        return [copy(LOF + q, late(a), late(a), lo)], [copy(CORE + 3 * CHUNKS + q, a, a, core)]

    def pass_on(copies):
        arrivals, sends = copies
        for c in arrivals:
            c.wait_recv()
        for c in sends:
            c.start()

    def ranged(q, f):
        @pl.when(jnp.logical_and(q >= 0, q < CHUNKS))
        def _():
            f(q)

    piece = column_piece(block, x, y, 0)
    source = hops == 0

    def column_arrival(i):
        copy(COL + i, piece, piece, core).wait_recv()

    def step(t, _):
        @pl.when(t == EARLY_LAG)
        def _():
            theirs = column_piece(block, x, y, 0, 2)
            column_arrival(0)
            for d in AROUND:
                copy(COL + 3 + d, theirs, theirs, device((x + d) % 4, y, z, k)).start()

        for i, d in enumerate(AROUND):
            @pl.when(jnp.logical_and(source, t == (i + 1) * HALVES))
            def _():
                column_arrival(d)

            @pl.when(jnp.logical_and(source, t == (i + 1) * HALVES + EARLY_LAG))
            def _():
                column_arrival(3 + d)

        other = 1 - near
        ranged(t, lambda q: relay_whole(near, q))
        ranged(t - EARLY_LAG, lambda q: relay_early(near, q))
        ranged(t - lag, lambda q: relay_whole(other, q))
        ranged(t - lag - EARLY_LAG, lambda q: relay_early(other, q))
        ranged(t - mine_lag - FAR_LAG, lambda q: pass_on(far_copies(q)))
        ranged(t - mine_lag - FAR_LAG, lambda q: pass_on(lo_copies(q)))
        ranged(t - mine_lag - LOF_LAG, lambda q: pass_on(lof_copies(q)))
        return 0

    lax.fori_loop(0, CHUNKS + max(LAGS) + LOF_LAG, step, 0)

    @pl.when(jnp.logical_not(source))
    def _():
        for i in range(1, 7):
            column_arrival(i)

    def end(q, _):
        for s in (0, 1):
            for _, _, _, copies in (whole_copies(s, q), early_copies(s, q)):
                for cond, c in copies:
                    when(cond, c.wait_send)
        for arrivals, sends in (far_copies(q), lo_copies(q), lof_copies(q)):
            for c in sends:
                c.wait_send()
        ref = full(lane, yh, q)
        for g in range(4):
            copy(CORE + g * CHUNKS + q, ref, ref, core).wait_recv()
        return 0

    lax.fori_loop(0, CHUNKS, end, 0)
    cp.finish()
    theirs = column_piece(block, x, y, 0, 2)
    for d in AROUND:
        copy(COL + 3 + d, theirs, theirs, core).wait_send()
    out = pltpu.make_async_copy(panel.at[pl.ds(0, 2048)], panel_out, sem)
    out.start()
    out.wait()


def split(a):
    hi = a.astype(BF16)
    return hi, (a - hi.astype(F32)).astype(BF16)


def dot3(ah, al, bh, bl, dims):
    d = lambda p, q: lax.dot_general(p, q, (dims, ((), ())), preferred_element_type=F32)
    return d(ah, bh) + (d(ah, bl) + d(al, bh))


TILE = 256
NN = ((1,), (0,))
NT = ((1,), (1,))


def first_partial_kernel(panel, omega, xh_out, xl_out, part, acc):
    i = pl.program_id(0)
    xh, xl = split(panel[...].T)
    xh_out[...] = xh
    xl_out[...] = xl
    oh, ol = split(omega[...])

    @pl.when(i == 0)
    def _():
        acc[...] = jnp.zeros_like(acc)

    acc[...] += dot3(xh, xl, oh, ol, NN)

    @pl.when(i == pl.num_programs(0) - 1)
    def _():
        part[...] = acc[...].T


def update_kernel(last, count, xr, yr, xc, yc, omega, xh, xl, *rest):
    if last:
        out, rh, rl = rest
    else:
        out, part, rh, rl, acc = rest
    i = pl.program_id(0)
    row0 = lax.axis_index("row") * 2048 + i * TILE
    col0 = lax.axis_index("col") * 512

    @pl.when(i == 0)
    def _():
        h, l = split(yc[...])
        rh[:, :S] = h
        rl[:, :S] = l
        h, l = split(xc[...])
        rh[:, S:] = h
        rl[:, S:] = l
        if not last:
            acc[...] = jnp.zeros_like(acc)

    ah, al = split(jnp.concatenate([xr[...], yr[...]], axis=1))
    cross = dot3(ah, al, rh[...], rl[...], NT)
    old = omega[...]
    moved = old - (STEP * 0.5 / count) * cross
    thr = STEP * PENALTY
    new = moved - jnp.clip(moved, -thr, thr)
    out[...] = new

    @pl.when(jnp.logical_and(row0 < col0 + 512, col0 < row0 + TILE))
    def _():
        gr = row0 + lax.broadcasted_iota(jnp.int32, (TILE, 512), 0)
        gc = col0 + lax.broadcasted_iota(jnp.int32, (TILE, 512), 1)
        on = gr == gc
        safe = jnp.where(on, old, 1.0)
        out[...] = jnp.where(on, moved + STEP / safe, new)

    if not last:
        nh, nl = split(out[...])
        acc[...] += dot3(xh[...], xl[...], nh, nl, NN)

        @pl.when(i == pl.num_programs(0) - 1)
        def _():
            part[...] = acc[...].T


def shape(*dims, dtype=F32):
    return jax.ShapeDtypeStruct(dims, dtype)


def vm():
    return pl.BlockSpec(memory_space=pltpu.VMEM)


def gather_samples(own):
    n = 48
    return pl.pallas_call(
        gather_samples_kernel,
        out_shape=(shape(2048, S), shape(512, S)),
        in_specs=[vm()], out_specs=(vm(), vm()),
        scratch_shapes=[pltpu.SemaphoreType.DMA((n,)), pltpu.SemaphoreType.DMA((n,)), pltpu.SemaphoreType.DMA],
        compiler_params=pltpu.CompilerParams(collective_id=0, has_side_effects=True, vmem_limit_bytes=VMEM_LIMIT),
        name="gather_samples",
    )(own)


def gather_projected(part):
    n = 14 + 16 * CHUNKS
    return pl.pallas_call(
        gather_projected_kernel,
        out_shape=(shape(2048, S), shape(512, S)),
        in_specs=[vm()], out_specs=(vm(), vm()),
        scratch_shapes=[pltpu.VMEM((2560, S), F32), pltpu.VMEM((7, 64, S), F32),
                        pltpu.SemaphoreType.DMA((n,)), pltpu.SemaphoreType.DMA((n,)), pltpu.SemaphoreType.DMA],
        compiler_params=pltpu.CompilerParams(collective_id=1, has_side_effects=True, vmem_limit_bytes=VMEM_LIMIT),
        name="gather_projected",
    )(part)


def first_partial(panel, omega):
    return pl.pallas_call(
        first_partial_kernel,
        grid=(2048 // TILE,),
        out_shape=(shape(S, 2048, dtype=BF16), shape(S, 2048, dtype=BF16), shape(512, S)),
        in_specs=[pl.BlockSpec((TILE, S), lambda i: (i, 0)), pl.BlockSpec((TILE, 512), lambda i: (i, 0))],
        out_specs=(pl.BlockSpec((S, TILE), lambda i: (0, i)), pl.BlockSpec((S, TILE), lambda i: (0, i)),
                   pl.BlockSpec((512, S), lambda i: (0, 0))),
        scratch_shapes=[pltpu.VMEM((S, 512), F32)],
        compiler_params=pltpu.CompilerParams(vmem_limit_bytes=VMEM_LIMIT),
        name="first_partial",
    )(panel, omega)


def update(last, xr, yr, xc, yc, omega, xh, xl):
    tile = pl.BlockSpec((TILE, S), lambda i: (i, 0))
    whole = pl.BlockSpec((512, S), lambda i: (0, 0))
    square = pl.BlockSpec((TILE, 512), lambda i: (i, 0))
    tall = pl.BlockSpec((S, TILE), lambda i: (0, i))
    scratch = [pltpu.VMEM((512, 2 * S), BF16), pltpu.VMEM((512, 2 * S), BF16)]
    if last:
        out_shape, out_specs = shape(2048, 512), square
    else:
        out_shape, out_specs = (shape(2048, 512), shape(512, S)), (square, whole)
        scratch.append(pltpu.VMEM((S, 512), F32))
    return pl.pallas_call(
        functools.partial(update_kernel, last, S),
        grid=(2048 // TILE,),
        out_shape=out_shape,
        in_specs=[tile, tile, whole, whole, square, tall, tall],
        out_specs=out_specs,
        scratch_shapes=scratch,
        compiler_params=pltpu.CompilerParams(vmem_limit_bytes=VMEM_LIMIT),
        name="update_last" if last else "update",
    )(xr, yr, xc, yc, omega, xh, xl)


def body(samples, omega):
    own = samples.T
    xr, xc = gather_samples(own)
    xh, xl, part = first_partial(xr, omega)
    yr, yc = gather_projected(part)
    omega, part = update(False, xr, yr, xc, yc, omega, xh, xl)
    yr, yc = gather_projected(part)
    return update(True, xr, yr, xc, yc, omega, xh, xl)


def solution(mesh):
    in_specs = (P(None, ("row", "col")), P("row", "col"))
    out_specs = P("row", "col")
    return jax.shard_map(body, mesh=mesh, in_specs=in_specs, out_specs=out_specs, check_vma=False)
```

```python
import jax
import jax.numpy as jnp
from jax import lax
from jax.experimental import pallas as pl
from jax.experimental.pallas import tpu as pltpu
from jax.sharding import PartitionSpec as P

ITERS = 2
STEP = 0.01
PENALTY = 0.25
S = 384
EARLY = 128
MESH = pl.DeviceIdType.MESH
F32 = jnp.float32
BF16 = jnp.bfloat16
VMEM_LIMIT = 56 * 2**20


def place():
    r = lax.axis_index("row")
    c = lax.axis_index("col")
    return r % 4, (r // 4) * 2 + (c // 2) % 2, c // 4, c % 2


def device(x, y, z, k):
    return (y // 2) * 4 + x, z * 4 + (y % 2) * 2 + k


def rows(start, size):
    return pl.ds(pl.multiple_of(start, 64), size)


class Copies:
    def __init__(self, send, recv):
        self.send, self.recv = send, recv
        self.pending = []

    def make(self, slot, src, dst, to):
        return pltpu.make_async_remote_copy(
            src_ref=src, dst_ref=dst, send_sem=self.send.at[slot], recv_sem=self.recv.at[slot],
            device_id=to, device_id_type=MESH)

    def start(self, slot, src, dst, to):
        copy = self.make(slot, src, dst, to)
        copy.start()
        self.pending.append((copy, None))
        return copy

    def start_if(self, cond, slot, src, dst, to, send=None):
        copy = pltpu.make_async_remote_copy(
            src_ref=src, dst_ref=dst, send_sem=self.send.at[slot if send is None else send],
            recv_sem=self.recv.at[slot], device_id=to, device_id_type=MESH)

        @pl.when(cond)
        def _():
            copy.start()

        self.pending.append((copy, cond))

    def finish(self):
        for copy, cond in self.pending:
            if cond is None:
                copy.wait_send()
            else:
                @pl.when(cond)
                def _():
                    copy.wait_send()


def column_piece(buf, x, y, d, e=0):
    return buf.at[rows((((y + e) % 4) // 2 * 4 + (x + 4 - d) % 4) * 64, 64)]


AROUND = (1, 3, 2)


def column_start(cp, buf, x, y, z, k, base):
    mine = column_piece(buf, x, y, 0)
    for d in AROUND:
        cp.start(base + d, mine, mine, device((x + d) % 4, y, z, k))
    cp.start(base, mine, mine, device(x, (y + 2) % 4, z, k))


def column_middle(cp, buf, x, y, z, k, base):
    theirs = column_piece(buf, x, y, 0, 2)
    cp.make(base, theirs, theirs, (0, 0)).wait_recv()
    for d in AROUND:
        cp.start(base + 3 + d, theirs, theirs, device((x + d) % 4, y, z, k))


def column_end(cp, buf, x, y, z, k, base):
    mine = column_piece(buf, x, y, 0)
    for d in AROUND:
        cp.make(base + d, mine, mine, (0, 0)).wait_recv()
        cp.make(base + 3 + d, mine, mine, (0, 0)).wait_recv()


CHUNK = 64
CHUNKS = 4
LAGS = (4, 2, 0)
EARLY_LAG = 1
FAR_LAG = EARLY_LAG + 1
LOF_LAG = FAR_LAG + 2
K3 = 6 * S
BLOCK = 256


def split(a):
    hi = a.astype(BF16)
    return hi, (a - hi.astype(F32)).astype(BF16)


def partial_block(i, acc, flipped, omega, right):
    hi, lo = split(omega[rows(i * BLOCK, BLOCK)])
    right[:BLOCK] = hi
    right[BLOCK:2 * BLOCK] = lo
    right[2 * BLOCK:] = hi
    acc[...] += jnp.dot(flipped[i], right[...], preferred_element_type=F32)


def flip_block(i, flipped, panel):
    hi, lo = split(panel[rows(i * BLOCK, BLOCK)].T)
    flipped[i, :, :BLOCK] = hi
    flipped[i, :, BLOCK:2 * BLOCK] = hi
    flipped[i, :, 2 * BLOCK:] = lo


def gather_samples(own_ref, panel, block, send, recv, where, partial):
    x, y, z, k = where
    yl, yh = y % 2, y // 2
    r, c = yh * 4 + x, z * 4 + yl * 2 + k
    up = device(x, y, (z + 1) % 8, k)
    down = device(x, y, (z + 7) % 8, k)
    lo = device(x, yh * 2 + 1 - yl, z, k)
    far = device(x, 3 - y, z, k)
    core = device(x, y, z, 1 - k)
    to_r, to_c = c % 8, r * 4 + c // 8
    own_b = c * 8 + r
    from_r, from_c = own_b // 32, own_b % 32
    moves = (to_r * 32 + to_c) != (r * 32 + c)
    group = [device((x + d) % 4, (y + e) % 4, z, k) for d in range(4) for e in (0, 2) if d or e]
    cp = Copies(send, recv)

    barrier = pltpu.get_barrier_semaphore()
    partners = [up, down, lo, far, core] + group
    for partner in partners:
        pl.semaphore_signal(barrier, inc=1, device_id=partner, device_id_type=MESH)

    @pl.when(moves)
    def _():
        pl.semaphore_signal(barrier, inc=1, device_id=(from_r, from_c), device_id_type=MESH)

    def at(zz, l):
        return panel.at[rows((zz * 4 + l * 2 + k) * 64, 64)]

    def early(ref):
        return ref.at[:, pl.ds(0, EARLY)]

    def late(ref):
        return ref.at[:, pl.ds(EARLY, S - EARLY)]

    panel[rows(c * 64, 64)] = own_ref[...]
    pl.semaphore_wait(barrier, len(partners) + jnp.where(moves, 1, 0))

    own = at(z, yl)
    E_OWN, UP, DOWN, UP_E, DOWN_E, LO, CORE, CORE_LO, COL = 0, 1, 5, 8, 12, 16, 24, 32, 40
    PERM = 47
    cp.start(E_OWN, early(own), early(own), lo)
    cp.start(UP, own, own, up)
    cp.start(DOWN, own, own, down)
    cp.start_if(moves, PERM, own, block.at[rows(to_r * 64, 64)], (to_r, to_c))

    @pl.when(jnp.logical_not(moves))
    def _():
        block[rows(r * 64, 64)] = own_ref[...]

    cp.start(LO, late(own), late(own), lo)
    cp.start(CORE, own, own, core)
    cp.make(E_OWN, early(own), early(own), lo).wait_recv()
    e = early(at(z, 1 - yl))
    cp.start(UP_E, e, e, up)
    cp.start(DOWN_E, e, e, down)

    def lo_arrived(i, zz):
        piece = at(zz, 1 - yl)
        cp.make(LO + i, late(piece), late(piece), lo).wait_recv()
        cp.start(CORE_LO + i, piece, piece, core)

    def multiply(i, zz):
        cp.make(CORE + i, own, own, core).wait_recv()
        cp.make(CORE_LO + i, own, own, core).wait_recv()
        partial(zz)

    for t in range(1, 5):
        a = at((z + 8 - t) % 8, yl)
        b = at((z + t) % 8, yl)
        cp.make(UP + t - 1, a, a, up).wait_recv()
        if t < 4:
            cp.start(UP + t, a, a, up)
            cp.make(DOWN + t - 1, b, b, down).wait_recv()
            if t < 3:
                cp.start(DOWN + t, b, b, down)
        ea = early(at((z + 8 - t) % 8, 1 - yl))
        eb = early(at((z + t) % 8, 1 - yl))
        if t < 4:
            cp.make(UP_E + t - 1, ea, ea, up).wait_recv()
            if t < 3:
                cp.start(UP_E + t, ea, ea, up)
        cp.make(DOWN_E + t - 1, eb, eb, down).wait_recv()
        if t < 4:
            cp.start(DOWN_E + t, eb, eb, down)
        cp.start(LO + 2 * t - 1, late(a), late(a), lo)
        cp.start(CORE + 2 * t - 1, a, a, core)
        if t < 4:
            cp.start(LO + 2 * t, late(b), late(b), lo)
            cp.start(CORE + 2 * t, b, b, core)
        if t == 2:
            @pl.when(moves)
            def _():
                cp.make(PERM, own, own, lo).wait_recv()

            column_start(cp, block, x, y, z, k, COL)
        if t == 3:
            column_middle(cp, block, x, y, z, k, COL)
        if t == 1:
            lo_arrived(0, z)
        else:
            lo_arrived(2 * t - 3, (z + 8 - (t - 1)) % 8)
            lo_arrived(2 * t - 2, (z + t - 1) % 8)
        if t == 2:
            multiply(0, z)
        if t > 2:
            multiply(2 * t - 5, (z + 8 - (t - 2)) % 8)
            multiply(2 * t - 4, (z + t - 2) % 8)
    multiply(5, (z + 5) % 8)
    lo_arrived(7, (z + 4) % 8)
    multiply(6, (z + 3) % 8)
    multiply(7, (z + 4) % 8)
    column_end(cp, block, x, y, z, k, COL)
    cp.finish()


def gather_projected(acc, part, block, panel, inbox, send, recv, where):
    x, y, z, k = where
    yl, yh = y % 2, y // 2
    r = yh * 4 + x
    up = device(x, y, (z + 1) % 8, k)
    down = device(x, y, (z + 7) % 8, k)
    lo = device(x, yh * 2 + 1 - yl, z, k)
    far = device(x, 3 - y, z, k)
    core = device(x, y, z, 1 - k)
    cp = Copies(send, recv)

    def scatter_copy(p):
        slot = (r + 7 - p) % 8
        return p != r, pltpu.make_async_remote_copy(
            src_ref=part.at[rows(p * 64, 64)], dst_ref=inbox.at[slot], send_sem=send.at[slot], recv_sem=recv.at[slot],
            device_id=device(p % 4, p // 4 * 2 + yl, z, k), device_id_type=MESH)

    for i in range(4):
        j = (r // 2 + 1 + i) % 4
        part[rows(j * 128, 128)] = acc[:, pl.ds(pl.multiple_of(j * 128, 128), 128)].T
        for p in (2 * j, 2 * j + 1):
            cond, c = scatter_copy(p)
            pl.when(cond)(c.start)
    total = part[rows(r * 64, 64)]
    for i in range(7):
        cp.make(i, inbox.at[i], inbox.at[i], core).wait_recv()
        total = total + inbox[i]
    block[rows(r * 64, 64)] = total
    COL = 7
    column_start(cp, block, x, y, z, k, COL)

    lane = (yl * 2 + k) * 512
    flane = ((1 - yl) * 2 + k) * 512
    fyh = 1 - yh

    def within(h, q):
        d = jnp.where(q == 2, 3, jnp.where(q == 3, 2, q))
        return h * 256 + (x + 4 - d) % 4 * 64

    def full(base, h, q):
        return panel.at[pl.ds(pl.multiple_of(base + within(h, q), CHUNK), CHUNK)]

    def early(ref):
        return ref.at[:, pl.ds(0, EARLY)]

    def late(ref):
        return ref.at[:, pl.ds(EARLY, S - EARLY)]

    d0 = (z + 8 - x) % 8
    near = jnp.where(jnp.logical_or(d0 <= 2, d0 >= 6), 0, 1)
    hops = (d0 + 4 * near) % 8
    hops = jnp.where(hops > 4, 8 - hops, hops)
    lag = jnp.where(hops == 0, LAGS[0], jnp.where(hops == 1, LAGS[1], LAGS[2]))
    mine_lag = jnp.where(near == yh, 0, lag)
    Z = 14
    ZD = Z + 4 * CHUNKS
    FAR = ZD + 4 * CHUNKS
    LO = FAR + 2 * CHUNKS
    LOF = LO + CHUNKS
    CORE = LOF + CHUNKS

    def copy(slot, src, dst, to, send_slot=None):
        return pltpu.make_async_remote_copy(
            src_ref=src, dst_ref=dst, send_sem=send.at[slot if send_slot is None else send_slot],
            recv_sem=recv.at[slot], device_id=to, device_id_type=MESH)

    def when(cond, f):
        pl.when(cond)(f)

    def at(base, h, q):
        return pl.ds(pl.multiple_of(base + within(h, q), CHUNK), CHUNK)

    def whole_copies(s, q):
        d = (d0 + 4 * s) % 8
        mine = s == yh
        ref = full(jnp.where(mine, lane, 2048), yh, q)
        to = full(lane, yh, q)
        slot = Z + (s * CHUNKS + q) * 2
        return d, ref, copy(slot, ref, ref, up), [
            (d <= 3, copy(slot, ref, ref, up)),
            (jnp.logical_or(d == 0, d >= 6), copy(slot, ref, ref, down, slot + ZD - Z)),
            (jnp.logical_not(mine), copy(FAR + 2 * q, ref, to, far)),
            (mine, copy(LO + q, late(to), late(to), lo)),
            (mine, copy(CORE + q, to, to, core)),
        ]

    def early_copies(s, q):
        d = (d0 + 4 * s) % 8
        mine = s == yh
        ref = early(full(jnp.where(mine, lane, 2048), fyh, q))
        to = early(full(lane, fyh, q))
        slot = Z + (s * CHUNKS + q) * 2 + 1
        return d, ref, copy(slot, ref, ref, up), [
            (d <= 2, copy(slot, ref, ref, up)),
            (jnp.logical_or(d == 0, d >= 5), copy(slot, ref, ref, down, slot + ZD - Z)),
            (jnp.logical_not(mine), copy(FAR + 2 * q + 1, ref, to, far)),
        ]

    def relay_whole(s, q):
        d, ref, arrival, copies = whole_copies(s, q)

        @pl.when(d == 0)
        def _():
            panel[at(jnp.where(s == yh, lane, 2048), yh, q)] = block[at(0, yh, q)]

        @pl.when(d != 0)
        def _():
            arrival.wait_recv()

        for cond, c in copies:
            when(cond, c.start)

    def relay_early(s, q):
        d, ref, arrival, copies = early_copies(s, q)

        @pl.when(d == 0)
        def _():
            panel[at(jnp.where(s == yh, lane, 2048), fyh, q), :EARLY] = block[at(0, fyh, q), :EARLY]

        @pl.when(d != 0)
        def _():
            arrival.wait_recv()

        for cond, c in copies:
            when(cond, c.start)

    def far_copies(q):
        a, b = full(flane, fyh, q), early(full(flane, yh, q))
        return [copy(FAR + 2 * q, a, a, far), copy(FAR + 2 * q + 1, b, b, far)], [
            copy(LOF + q, late(a), late(a), lo), copy(CORE + CHUNKS + q, a, a, core)]

    def lo_copies(q):
        a = full(flane, yh, q)
        return [copy(LO + q, late(a), late(a), lo)], [copy(CORE + 2 * CHUNKS + q, a, a, core)]

    def lof_copies(q):
        a = full(lane, fyh, q)
        return [copy(LOF + q, late(a), late(a), lo)], [copy(CORE + 3 * CHUNKS + q, a, a, core)]

    def pass_on(copies):
        arrivals, sends = copies
        for c in arrivals:
            c.wait_recv()
        for c in sends:
            c.start()

    def ranged(q, f):
        @pl.when(jnp.logical_and(q >= 0, q < CHUNKS))
        def _():
            f(q)

    piece = column_piece(block, x, y, 0)
    source = hops == 0

    def column_arrival(i):
        copy(COL + i, piece, piece, core).wait_recv()

    def step(t, _):
        @pl.when(t == EARLY_LAG)
        def _():
            theirs = column_piece(block, x, y, 0, 2)
            column_arrival(0)
            for d in AROUND:
                copy(COL + 3 + d, theirs, theirs, device((x + d) % 4, y, z, k)).start()

        for i, d in enumerate(AROUND):
            @pl.when(jnp.logical_and(source, t == i + 1))
            def _():
                column_arrival(d)

            @pl.when(jnp.logical_and(source, t == i + 1 + EARLY_LAG))
            def _():
                column_arrival(3 + d)

        other = 1 - near
        ranged(t, lambda q: relay_whole(near, q))
        ranged(t - EARLY_LAG, lambda q: relay_early(near, q))
        ranged(t - lag, lambda q: relay_whole(other, q))
        ranged(t - lag - EARLY_LAG, lambda q: relay_early(other, q))
        ranged(t - mine_lag - FAR_LAG, lambda q: pass_on(far_copies(q)))
        ranged(t - mine_lag - FAR_LAG, lambda q: pass_on(lo_copies(q)))
        ranged(t - mine_lag - LOF_LAG, lambda q: pass_on(lof_copies(q)))
        return 0

    lax.fori_loop(0, CHUNKS + max(LAGS) + LOF_LAG, step, 0)

    @pl.when(jnp.logical_not(source))
    def _():
        for i in range(1, 7):
            column_arrival(i)

    def end(q, _):
        for s in (0, 1):
            for _, _, _, copies in (whole_copies(s, q), early_copies(s, q)):
                for cond, c in copies:
                    when(cond, c.wait_send)
        for arrivals, sends in (far_copies(q), lo_copies(q), lof_copies(q)):
            for c in sends:
                c.wait_send()
        ref = full(lane, yh, q)
        for g in range(4):
            copy(CORE + g * CHUNKS + q, ref, ref, core).wait_recv()
        return 0

    lax.fori_loop(0, CHUNKS, end, 0)
    cp.finish()
    theirs = column_piece(block, x, y, 0, 2)
    for d in AROUND:
        copy(COL + 3 + d, theirs, theirs, core).wait_send()
    for p in range(8):
        cond, c = scatter_copy(p)
        pl.when(cond)(c.wait_send)


TILE = 512


def update_tile(i, where, count, samples, projected, omega, left, right):
    x, y, z, k = where
    at = rows(i * TILE, TILE)
    for j, ref in enumerate((samples, projected)):
        hi, lo = split(ref[at])
        left[:, j * S:(j + 1) * S] = hi
        left[:, (j + 2) * S:(j + 3) * S] = hi
        left[:, (j + 4) * S:(j + 5) * S] = lo
    cross = lax.dot_general(left[...], right[...], (((1,), (1,)), ((), ())), preferred_element_type=F32)
    old = omega[at]
    moved = old - (STEP * 0.5 / count) * cross
    threshold = STEP * PENALTY
    new = moved - jnp.clip(moved, -threshold, threshold)
    omega[at] = new

    @pl.when(((y // 2) * 4 + x) * 4 + i == z * 4 + (y % 2) * 2 + k)
    def _():
        shape = (TILE, TILE)
        on = lax.broadcasted_iota(jnp.int32, shape, 0) == lax.broadcasted_iota(jnp.int32, shape, 1)
        safe = jnp.where(on, old, 1.0)
        omega[at] = jnp.where(on, moved + STEP / safe, new)


def set_right(right, block, first):
    hi, lo = split(block[...])
    right[:, first * S:(first + 1) * S] = hi
    right[:, (first + 2) * S:(first + 3) * S] = lo
    right[:, (first + 4) * S:(first + 5) * S] = hi


def kernel(own_ref, omega_ref, out_ref, omega, samples, samples_block, flipped, acc, part, projected0, projected1,
           block0, block1, inbox0, inbox1, left, right, tall, x_send, x_recv, send0, recv0, send1, recv1, in_sem, out_sem):
    where = place()
    load = pltpu.make_async_copy(omega_ref, omega, in_sem)
    load.start()
    acc[...] = jnp.zeros_like(acc)
    loaded = []

    def partial(zz):
        flip_block(zz, flipped, samples)
        if not loaded:
            load.wait()
            loaded.append(True)
        partial_block(zz, acc, flipped, omega, tall)

    gather_samples(own_ref, samples, samples_block, x_send, x_recv, where, partial)
    gather_projected(acc, part, block0, projected0, inbox0, send0, recv0, where)
    set_right(right, samples_block, 1)
    set_right(right, block0, 0)
    acc[...] = jnp.zeros_like(acc)

    def first(i, _):
        update_tile(i, where, S, samples, projected0, omega, left, right)
        partial_block(2 * i, acc, flipped, omega, tall)
        partial_block(2 * i + 1, acc, flipped, omega, tall)
        return 0

    lax.fori_loop(0, 2048 // TILE, first, 0)
    gather_projected(acc, part, block1, projected1, inbox1, send1, recv1, where)
    set_right(right, block1, 0)

    def store(i):
        at = rows(i * TILE, TILE)
        return pltpu.make_async_copy(omega.at[at], out_ref.at[at], out_sem.at[i])

    def second(i, _):
        update_tile(i, where, S, samples, projected1, omega, left, right)
        store(i).start()
        return 0

    lax.fori_loop(0, 2048 // TILE, second, 0)
    for i in range(2048 // TILE):
        store(i).wait()


def body(samples, omega):
    n = 14 + 16 * CHUNKS
    dma = pltpu.SemaphoreType.DMA
    vmem = pltpu.VMEM
    return pl.pallas_call(
        kernel,
        out_shape=jax.ShapeDtypeStruct((2048, 512), F32),
        in_specs=[pl.BlockSpec(memory_space=pltpu.VMEM), pl.BlockSpec(memory_space=pl.ANY)],
        out_specs=pl.BlockSpec(memory_space=pl.ANY),
        scratch_shapes=[
            vmem((2048, 512), F32), vmem((2048, S), F32), vmem((512, S), F32), vmem((8, S, 3 * BLOCK), BF16),
            vmem((S, 512), F32), vmem((512, S), F32), vmem((2560, S), F32), vmem((2560, S), F32),
            vmem((512, S), F32), vmem((512, S), F32), vmem((7, 64, S), F32), vmem((7, 64, S), F32),
            vmem((TILE, K3), BF16), vmem((512, K3), BF16), vmem((3 * BLOCK, 512), BF16),
            dma((48,)), dma((48,)), dma((n,)), dma((n,)), dma((n,)), dma((n,)), dma, dma((2048 // TILE,)),
        ],
        compiler_params=pltpu.CompilerParams(collective_id=0, has_side_effects=True, vmem_limit_bytes=VMEM_LIMIT),
        name="concord_steps",
    )(samples.T, omega)


def solution(mesh):
    in_specs = (P(None, ("row", "col")), P("row", "col"))
    out_specs = P("row", "col")
    return jax.shard_map(body, mesh=mesh, in_specs=in_specs, out_specs=out_specs, check_vma=False)
```

```python
import jax
import jax.numpy as jnp
from jax import lax
from jax.experimental import pallas as pl
from jax.experimental.pallas import tpu as pltpu
from jax.sharding import PartitionSpec as P

ITERS = 2
STEP = 0.01
PENALTY = 0.25
S = 384
EARLY = 128
MESH = pl.DeviceIdType.MESH
F32 = jnp.float32
BF16 = jnp.bfloat16
VMEM_LIMIT = 58 * 2**20


def place():
    r = lax.axis_index("row")
    c = lax.axis_index("col")
    return r % 4, (r // 4) * 2 + (c // 2) % 2, c // 4, c % 2


def device(x, y, z, k):
    return (y // 2) * 4 + x, z * 4 + (y % 2) * 2 + k


def rows(start, size):
    return pl.ds(pl.multiple_of(start, 64), size)


def copy(src, dst, send, recv, to):
    return pltpu.make_async_remote_copy(
        src_ref=src, dst_ref=dst, send_sem=send, recv_sem=recv, device_id=to, device_id_type=MESH)


class Copies:
    def __init__(self, send, recv):
        self.send, self.recv = send, recv

    def make(self, slot, src, dst, to):
        return copy(src, dst, self.send, self.recv.at[slot], to)

    def start(self, slot, src, dst, to):
        self.make(slot, src, dst, to).start()


def column_piece(buf, x, y, d, e=0):
    return buf.at[rows((((y + e) % 4) // 2 * 4 + (x + 4 - d) % 4) * 64, 64)]


AROUND = (1, 3, 2)


def column_start(cp, buf, x, y, z, k, base):
    mine = column_piece(buf, x, y, 0)
    for d in AROUND:
        cp.start(base + d, mine, mine, device((x + d) % 4, y, z, k))
    cp.start(base, mine, mine, device(x, (y + 2) % 4, z, k))


def column_middle(cp, buf, x, y, z, k, base):
    theirs = column_piece(buf, x, y, 0, 2)
    cp.make(base, theirs, theirs, (0, 0)).wait_recv()
    for d in AROUND:
        cp.start(base + 3 + d, theirs, theirs, device((x + d) % 4, y, z, k))


PARTS = 1
CHUNK = 64 // PARTS
CHUNKS = 4 * PARTS
HOP = 1.6
EARLY_LAG = 0.3
K3 = 6 * S
BLOCK = 256


def split(a):
    hi = a.astype(BF16)
    return hi, (a - hi.astype(F32)).astype(BF16)


def partial_block(i, acc, flipped, omega, right):
    hi, lo = split(omega[rows(i * BLOCK, BLOCK)])
    right[:BLOCK] = hi
    right[BLOCK:2 * BLOCK] = lo
    right[2 * BLOCK:] = hi
    acc[...] += jnp.dot(flipped[i], right[...], preferred_element_type=F32)


def flip_block(i, flipped, panel):
    hi, lo = split(panel[rows(i * BLOCK, BLOCK)].T)
    flipped[i, :, :BLOCK] = hi
    flipped[i, :, BLOCK:2 * BLOCK] = hi
    flipped[i, :, 2 * BLOCK:] = lo


def gather_samples(own_ref, panel, block, measure, send, recv, where, partial):
    x, y, z, k = where
    yl, yh = y % 2, y // 2
    r, c = yh * 4 + x, z * 4 + yl * 2 + k
    up = device(x, y, (z + 1) % 8, k)
    down = device(x, y, (z + 7) % 8, k)
    lo = device(x, yh * 2 + 1 - yl, z, k)
    far = device(x, 3 - y, z, k)
    core = device(x, y, z, 1 - k)
    to_r, to_c = c % 8, r * 4 + c // 8
    own_b = c * 8 + r
    from_r, from_c = own_b // 32, own_b % 32
    moves = (to_r * 32 + to_c) != (r * 32 + c)
    group = [device((x + d) % 4, (y + e) % 4, z, k) for d in range(4) for e in (0, 2) if d or e]
    cp = Copies(send.at[0], recv)

    barrier = pltpu.get_barrier_semaphore()
    partners = [up, down, lo, far, core] + group
    for partner in partners:
        pl.semaphore_signal(barrier, inc=1, device_id=partner, device_id_type=MESH)

    @pl.when(moves)
    def _():
        pl.semaphore_signal(barrier, inc=1, device_id=(from_r, from_c), device_id_type=MESH)

    def at(zz, l):
        return panel.at[rows((zz * 4 + l * 2 + k) * 64, 64)]

    def early(ref):
        return ref.at[:, pl.ds(0, EARLY)]

    def late(ref):
        return ref.at[:, pl.ds(EARLY, S - EARLY)]

    def half(ref, h):
        return ref.at[pl.ds(h * 32, 32)]

    panel[rows(c * 64, 64)] = own_ref[...]
    pl.semaphore_wait(barrier, len(partners) + jnp.where(moves, 1, 0))

    own = at(z, yl)
    E_OWN, UP, DOWN, UP_E, DOWN_E, LO, CORE, CORE_LO, COL = 0, 48, 56, 8, 12, 16, 24, 32, 40
    PERM = 47
    cp.start(E_OWN, early(own), early(own), lo)
    for h in (0, 1):
        cp.start(UP + h, half(own, h), half(own, h), up)
        cp.start(DOWN + h, half(own, h), half(own, h), down)
    permuted = copy(own, block.at[rows(to_r * 64, 64)], send.at[1], recv.at[PERM], (to_r, to_c))
    pl.when(moves)(permuted.start)

    @pl.when(jnp.logical_not(moves))
    def _():
        block[rows(r * 64, 64)] = own_ref[...]

    cp.start(LO, late(own), late(own), lo)
    cp.start(CORE, own, own, core)
    cp.make(E_OWN, early(own), early(own), lo).wait_recv()
    e = early(at(z, 1 - yl))
    cp.start(UP_E, e, e, up)
    cp.start(DOWN_E, e, e, down)

    def lo_arrived(i, zz):
        piece = at(zz, 1 - yl)
        cp.make(LO + i, late(piece), late(piece), lo).wait_recv()
        cp.start(CORE_LO + i, piece, piece, core)

    def relay(slot, ref, to, more):
        for h in (0, 1):
            part = half(ref, h)
            cp.make(slot + h, part, part, to).wait_recv()
            if more:
                cp.start(slot + 2 + h, part, part, to)

    def multiply(i, zz):
        cp.make(CORE + i, own, own, core).wait_recv()
        cp.make(CORE_LO + i, own, own, core).wait_recv()
        partial(zz)

    for t in range(1, 5):
        a = at((z + 8 - t) % 8, yl)
        b = at((z + t) % 8, yl)
        relay(UP + 2 * t - 2, a, up, t < 4)
        if t < 4:
            relay(DOWN + 2 * t - 2, b, down, t < 3)
        ea = early(at((z + 8 - t) % 8, 1 - yl))
        eb = early(at((z + t) % 8, 1 - yl))
        if t < 4:
            cp.make(UP_E + t - 1, ea, ea, up).wait_recv()
            if t < 3:
                cp.start(UP_E + t, ea, ea, up)
        cp.make(DOWN_E + t - 1, eb, eb, down).wait_recv()
        if t < 4:
            cp.start(DOWN_E + t, eb, eb, down)
        cp.start(LO + 2 * t - 1, late(a), late(a), lo)
        cp.start(CORE + 2 * t - 1, a, a, core)
        if t < 4:
            cp.start(LO + 2 * t, late(b), late(b), lo)
            cp.start(CORE + 2 * t, b, b, core)
        if t == 2:
            @pl.when(moves)
            def _():
                cp.make(PERM, own, own, lo).wait_recv()

            column_start(cp, block, x, y, z, k, COL)
        if t == 3:
            column_middle(cp, block, x, y, z, k, COL)
        if t == 1:
            lo_arrived(0, z)
        else:
            lo_arrived(2 * t - 3, (z + 8 - (t - 1)) % 8)
            lo_arrived(2 * t - 2, (z + t - 1) % 8)
        if t == 2:
            multiply(0, z)
        if t > 2:
            multiply(2 * t - 5, (z + 8 - (t - 2)) % 8)
            multiply(2 * t - 4, (z + t - 2) % 8)
    lo_arrived(7, (z + 4) % 8)
    multiply(5, (z + 5) % 8)
    multiply(6, (z + 3) % 8)
    multiply(7, (z + 4) % 8)
    for i in range(1, 7):
        cp.make(COL + i, own, own, core).wait_recv()

    def finish():
        sent = measure.at[pl.ds(0, 38 * 64)]
        cp.make(0, sent, sent, core).wait_send()
        pl.when(moves)(permuted.wait_send)

    return finish


def timetable(hops, near_is_mine):
    base = {"near": HOP * hops, "other": HOP * (4 - hops)}
    mine = base["near" if near_is_mine else "other"]
    events = [(1.5 * PARTS, 7, "column start", 0), (3.5 * PARTS, 7, "column middle", 0)]
    for q in range(CHUNKS):
        for n, stream in enumerate(("near", "other")):
            events.append((base[stream] + q, 1 + n, stream + " whole", q))
            events.append((base[stream] + q + EARLY_LAG, 1 + n, stream + " early", q))
        events.append((mine + q + HOP, 3, "far whole", q))
        events.append((mine + q + EARLY_LAG + HOP, 4, "far early", q))
        events.append((mine + q + EARLY_LAG + 0.1 + HOP, 5, "lo", q))
        events.append((mine + q + max(2 * HOP, EARLY_LAG + 0.1), 6, "lo far", q))
    return [(name, q) for _, _, name, q in sorted(events)]


RS, CORE, COL, Z, FAR, LO, LOF = 0, 1, 2, 9, 9 + 4 * CHUNKS, 9 + 6 * CHUNKS, 9 + 7 * CHUNKS
FED = 9 + 8 * CHUNKS
RECVS = FED + 4
S_RS, S_CORE, S_COL, S_NEAR, S_SOURCE, S_OTHER, S_FAR, S_LO, S_FED = 0, 1, 2, 3, 5, 7, 9, 11, 12
SENDS = 13


def gather_projected(acc, part, block, panel, inbox, fed, send, recv, where, meanwhile):
    x, y, z, k = where
    yl, yh = y % 2, y // 2
    r = yh * 4 + x
    up = device(x, y, (z + 1) % 8, k)
    down = device(x, y, (z + 7) % 8, k)
    lo = device(x, yh * 2 + 1 - yl, z, k)
    far = device(x, 3 - y, z, k)
    core = device(x, y, z, 1 - k)

    for i in range(4):
        j = (r // 2 + 1 + i) % 4
        part[rows(j * 128, 128)] = acc[:, pl.ds(pl.multiple_of(j * 128, 128), 128)].T
        for p in (2 * j, 2 * j + 1):
            c = copy(part.at[rows(p * 64, 64)], inbox.at[rows((r + 7 - p) % 8 * 64, 64)], send.at[S_RS], recv.at[RS],
                     device(p % 4, p // 4 * 2 + yl, z, k))
            pl.when(p != r)(c.start)
    meanwhile()
    copy(inbox, inbox, send.at[S_RS], recv.at[RS], core).wait_recv()
    total = part[rows(r * 64, 64)]
    for i in range(7):
        total = total + inbox[i * 64:(i + 1) * 64]
    block[rows(r * 64, 64)] = total
    column = Copies(send.at[S_COL], recv)
    piece = column_piece(block, x, y, 0)

    def column_arrival(i):
        column.make(COL + i, piece, piece, core).wait_recv()

    xs = z % 4
    to_source = copy(piece, piece, send.at[S_COL], recv.at[COL + (xs + 4 - x) % 4], device(xs, y, z, k))
    pl.when(x != xs)(to_source.start)
    extra = copy(piece.at[:, pl.ds(0, EARLY)], fed.at[rows(x * 64, 64)], send.at[S_FED], recv.at[FED + x],
                 device(xs, (y + 2) % 4, z, k))
    extra.start()

    def fed_arrival(d):
        at = (x + 4 - d) % 4
        ref = fed.at[rows(at * 64, 64)]
        copy(ref, ref, send.at[S_FED], recv.at[FED + at], core).wait_recv()

    def column_start():
        for d in AROUND:
            c = column.make(COL + d, piece, piece, device((x + d) % 4, y, z, k))
            pl.when((x + d) % 4 != xs)(c.start)
        column.start(COL, piece, piece, device(x, (y + 2) % 4, z, k))

    lane = (yl * 2 + k) * 512
    flane = ((1 - yl) * 2 + k) * 512
    fyh = 1 - yh
    around = [(x + 4 - d) % 4 * 64 + i * CHUNK for d in (0,) + AROUND for i in range(PARTS)]
    within = {"own": [yh * 256 + a for a in around], "far": [fyh * 256 + a for a in around]}

    def chunk(base, half, q):
        return pl.ds(pl.multiple_of(base + within[half][q], CHUNK), CHUNK)

    def whole(base, half, q):
        return panel.at[chunk(base, half, q)]

    def early(ref):
        return ref.at[:, pl.ds(0, EARLY)]

    def late(ref):
        return ref.at[:, pl.ds(EARLY, S - EARLY)]

    d0 = (z + 8 - x) % 8
    near = jnp.where(jnp.logical_or(d0 <= 2, d0 >= 6), 0, 1)
    d = (d0 + 4 * near) % 8
    rising = d <= 2
    on = tuple(jnp.where(rising, a, b) for a, b in zip(up, down))
    back = tuple(jnp.where(rising, b, a) for a, b in zip(up, down))
    hops = jnp.where(rising, d, 8 - d)
    near_is_mine = near == yh

    def run(h, near_mine):
        def relay(stream, kind, q):
            n = 0 if kind == "whole" else 1
            mine = (stream == "near") == near_mine
            base = lane if mine else 2048
            half = "own" if kind == "whole" else "far"
            cut = (lambda ref: ref) if kind == "whole" else early
            ref = cut(whole(base, half, q))
            slot = recv.at[Z + ((0 if mine else 1) * CHUNKS + q) * 2 + n]
            source = stream == "near" and h == 0
            if source:
                dist = ((0,) + AROUND)[q // PARTS]
                if kind == "whole":
                    if q and q % PARTS == 0:
                        column_arrival(dist)
                    panel[chunk(base, half, q)] = block[chunk(0, half, q)]
                else:
                    if q % PARTS == 0:
                        fed_arrival(dist)
                    at = pl.ds(pl.multiple_of(around[q], CHUNK), CHUNK)
                    panel[chunk(base, half, q), :EARLY] = fed[at]
                copy(ref, ref, send.at[S_SOURCE + n], slot, down).start()
            else:
                copy(ref, ref, send.at[S_NEAR], slot, core).wait_recv()
            if stream == "near":
                copy(ref, ref, send.at[S_NEAR + n], slot, on).start()
            elif h > 0:
                c = copy(ref, ref, send.at[S_OTHER + n], slot, back)
                if h == 2:
                    c.start()
                else:
                    pl.when(jnp.logical_not(rising) if kind == "whole" else rising)(c.start)
            if not mine:
                copy(ref, cut(whole(lane, half, q)), send.at[S_FAR + n], recv.at[FAR + 2 * q + n], far).start()
            elif kind == "whole":
                copy(late(ref), late(ref), send.at[S_LO], recv.at[LO + q], lo).start()
                copy(ref, ref, send.at[S_CORE], recv.at[CORE], core).start()

        def arrive(ref, slot):
            copy(ref, ref, send.at[S_CORE], recv.at[slot], core).wait_recv()

        def to_core(ref):
            copy(ref, ref, send.at[S_CORE], recv.at[CORE], core).start()

        for name, q in timetable(h, near_mine):
            if name == "column start":
                column_start()
            elif name == "column middle":
                column_middle(column, block, x, y, z, k, COL)
            elif name == "far whole":
                ref = whole(flane, "far", q)
                arrive(ref, FAR + 2 * q)
                copy(late(ref), late(ref), send.at[S_LO], recv.at[LOF + q], lo).start()
                to_core(ref)
            elif name == "far early":
                arrive(early(whole(flane, "own", q)), FAR + 2 * q + 1)
            elif name == "lo":
                ref = whole(flane, "own", q)
                arrive(late(ref), LO + q)
                to_core(ref)
            elif name == "lo far":
                ref = whole(lane, "far", q)
                arrive(late(ref), LOF + q)
                to_core(ref)
            else:
                relay(*name.split(), q)
        for i in range(1 if h else 4, 7):
            column_arrival(i)

    for h in (0, 1, 2):
        for near_mine in (True, False):
            pl.when(jnp.logical_and(hops == h, near_is_mine if near_mine else jnp.logical_not(near_is_mine)))(
                lambda h=h, near_mine=near_mine: run(h, near_mine))

    def sized(n, columns=S):
        return panel.at[pl.ds(0, n), pl.ds(0, columns)]

    got = sized(1024)
    copy(got, got, send.at[S_CORE], recv.at[CORE], core).wait_recv()

    def finish():
        def sent(slot, ref, cond=None):
            c = copy(ref, ref, send.at[slot], recv.at[RS], core)
            if cond is None:
                c.wait_send()
            else:
                pl.when(cond)(c.wait_send)

        sent(S_RS, sized(448))
        sent(S_COL, sized(448))
        sent(S_CORE, got)
        sent(S_LO, sized(512, S - EARLY))
        sent(S_FED, sized(64, EARLY))
        for n, ref in enumerate((sized(256), sized(256, EARLY))):
            sent(S_NEAR + n, ref)
            sent(S_FAR + n, ref)
            sent(S_SOURCE + n, ref, hops == 0)
            sent(S_OTHER + n, ref, jnp.logical_or(hops == 2, jnp.logical_and(
                hops == 1, rising if n else jnp.logical_not(rising))))

    return finish


TILE = 512


def update_tile(i, where, count, samples, projected, omega, left, right):
    x, y, z, k = where
    at = rows(i * TILE, TILE)
    for j, ref in enumerate((samples, projected)):
        hi, lo = split(ref[at])
        left[:, j * S:(j + 1) * S] = hi
        left[:, (j + 2) * S:(j + 3) * S] = hi
        left[:, (j + 4) * S:(j + 5) * S] = lo
    cross = lax.dot_general(left[...], right[...], (((1,), (1,)), ((), ())), preferred_element_type=F32)
    old = omega[at]
    moved = old - (STEP * 0.5 / count) * cross
    threshold = STEP * PENALTY
    new = moved - jnp.clip(moved, -threshold, threshold)
    omega[at] = new

    @pl.when(((y // 2) * 4 + x) * 4 + i == z * 4 + (y % 2) * 2 + k)
    def _():
        shape = (TILE, TILE)
        on = lax.broadcasted_iota(jnp.int32, shape, 0) == lax.broadcasted_iota(jnp.int32, shape, 1)
        safe = jnp.where(on, old, 1.0)
        omega[at] = jnp.where(on, moved + STEP / safe, new)


def set_right(right, block, first):
    hi, lo = split(block[...])
    right[:, first * S:(first + 1) * S] = hi
    right[:, (first + 2) * S:(first + 3) * S] = lo
    right[:, (first + 4) * S:(first + 5) * S] = hi


def kernel(own_ref, omega_ref, omega, samples, samples_block, flipped, acc, part, part1, projected0, projected1,
           block0, block1, inbox0, inbox1, fed0, fed1, left, right, tall, x_send, x_recv, send0, recv0, send1, recv1, in_sem):
    where = place()
    load = pltpu.make_async_copy(omega_ref, omega, in_sem)
    load.start()
    acc[...] = jnp.zeros_like(acc)
    loaded = []

    def partial(zz):
        flip_block(zz, flipped, samples)
        if not loaded:
            load.wait()
            loaded.append(True)
        partial_block(zz, acc, flipped, omega, tall)

    finish = gather_samples(own_ref, samples, samples_block, projected0, x_send, x_recv, where, partial)
    finish = gather_projected(acc, part, block0, projected0, inbox0, fed0, send0, recv0, where, finish)
    set_right(right, samples_block, 1)
    set_right(right, block0, 0)
    acc[...] = jnp.zeros_like(acc)

    def first(i, _):
        update_tile(i, where, S, samples, projected0, omega, left, right)
        partial_block(2 * i, acc, flipped, omega, tall)
        partial_block(2 * i + 1, acc, flipped, omega, tall)
        return 0

    lax.fori_loop(0, 2048 // TILE, first, 0)
    finish = gather_projected(acc, part1, block1, projected1, inbox1, fed1, send1, recv1, where, finish)
    set_right(right, block1, 0)

    def second(i, _):
        update_tile(i, where, S, samples, projected1, omega, left, right)
        return 0

    lax.fori_loop(0, 2048 // TILE, second, 0)
    finish()


def body(samples, omega):
    dma = pltpu.SemaphoreType.DMA
    vmem = pltpu.VMEM
    return pl.pallas_call(
        kernel,
        out_shape=pltpu.VMEM((2048, 512), F32),
        in_specs=[pl.BlockSpec(memory_space=pltpu.VMEM), pl.BlockSpec(memory_space=pltpu.HBM)],
        out_specs=pl.BlockSpec(memory_space=pltpu.VMEM),
        scratch_shapes=[
            vmem((2048, S), F32), vmem((512, S), F32), vmem((8, S, 3 * BLOCK), BF16),
            vmem((S, 512), F32), vmem((512, S), F32), vmem((512, S), F32), vmem((2560, S), F32), vmem((2560, S), F32),
            vmem((512, S), F32), vmem((512, S), F32), vmem((7 * 64, S), F32), vmem((7 * 64, S), F32), vmem((256, EARLY), F32), vmem((256, EARLY), F32),
            vmem((TILE, K3), BF16), vmem((512, K3), BF16), vmem((3 * BLOCK, 512), BF16),
            dma((2,)), dma((62,)), dma((SENDS,)), dma((RECVS,)), dma((SENDS,)), dma((RECVS,)), dma,
        ],
        compiler_params=pltpu.CompilerParams(collective_id=0, has_side_effects=True, vmem_limit_bytes=VMEM_LIMIT),
        name="concord_steps",
    )(samples.T, omega)


def solution(mesh):
    in_specs = (P(None, ("row", "col")), P("row", "col"))
    out_specs = P("row", "col")
    return jax.shard_map(body, mesh=mesh, in_specs=in_specs, out_specs=out_specs, check_vma=False)
```

```python
import jax
import jax.numpy as jnp
from jax import lax
from jax.experimental import pallas as pl
from jax.experimental.pallas import tpu as pltpu
from jax.sharding import PartitionSpec as P

ITERS = 2
STEP = 0.01
PENALTY = 0.25
S = 384
EARLY = 128
MESH = pl.DeviceIdType.MESH
F32 = jnp.float32
BF16 = jnp.bfloat16
VMEM_LIMIT = 58 * 2**20


def place():
    r = lax.axis_index("row")
    c = lax.axis_index("col")
    return r % 4, (r // 4) * 2 + (c // 2) % 2, c // 4, c % 2


def device(x, y, z, k):
    return (y // 2) * 4 + x, z * 4 + (y % 2) * 2 + k


def rows(start, size):
    return pl.ds(pl.multiple_of(start, 64), size)


def copy(src, dst, send, recv, to):
    return pltpu.make_async_remote_copy(
        src_ref=src, dst_ref=dst, send_sem=send, recv_sem=recv, device_id=to, device_id_type=MESH)


class Copies:
    def __init__(self, send, recv):
        self.send, self.recv = send, recv

    def make(self, slot, src, dst, to):
        return copy(src, dst, self.send, self.recv.at[slot], to)

    def start(self, slot, src, dst, to):
        self.make(slot, src, dst, to).start()


def column_piece(buf, x, y, d, e=0):
    return buf.at[rows((((y + e) % 4) // 2 * 4 + (x + 4 - d) % 4) * 64, 64)]


AROUND = (1, 3, 2)


def column_start(cp, buf, x, y, z, k, base):
    mine = column_piece(buf, x, y, 0)
    for d in AROUND:
        cp.start(base + d, mine, mine, device((x + d) % 4, y, z, k))
    cp.start(base, mine, mine, device(x, (y + 2) % 4, z, k))


def column_middle(cp, buf, x, y, z, k, base):
    theirs = column_piece(buf, x, y, 0, 2)
    cp.make(base, theirs, theirs, (0, 0)).wait_recv()
    for d in AROUND:
        cp.start(base + 3 + d, theirs, theirs, device((x + d) % 4, y, z, k))


CHUNK = 64
CHUNKS = 4
HOP = 2.1
LATE = 4.0
K3 = 6 * S
BLOCK = 256


def split(a):
    hi = a.astype(BF16)
    return hi, (a - hi.astype(F32)).astype(BF16)


def partial_block(i, acc, flipped, omega, right):
    hi, lo = split(omega[rows(i * BLOCK, BLOCK)])
    right[:BLOCK] = hi
    right[BLOCK:2 * BLOCK] = lo
    right[2 * BLOCK:] = hi
    acc[...] += jnp.dot(flipped[i], right[...], preferred_element_type=F32)


def flip_block(i, flipped, panel):
    hi, lo = split(panel[rows(i * BLOCK, BLOCK)].T)
    flipped[i, :, :BLOCK] = hi
    flipped[i, :, BLOCK:2 * BLOCK] = hi
    flipped[i, :, 2 * BLOCK:] = lo


def gather_samples(own_ref, panel, block, measure, send, recv, where, partial):
    x, y, z, k = where
    yl, yh = y % 2, y // 2
    r, c = yh * 4 + x, z * 4 + yl * 2 + k
    up = device(x, y, (z + 1) % 8, k)
    down = device(x, y, (z + 7) % 8, k)
    lo = device(x, yh * 2 + 1 - yl, z, k)
    far = device(x, 3 - y, z, k)
    core = device(x, y, z, 1 - k)
    to_r, to_c = c % 8, r * 4 + c // 8
    own_b = c * 8 + r
    from_r, from_c = own_b // 32, own_b % 32
    moves = (to_r * 32 + to_c) != (r * 32 + c)
    group = [device((x + d) % 4, (y + e) % 4, z, k) for d in range(4) for e in (0, 2) if d or e]
    cp = Copies(send.at[0], recv)

    barrier = pltpu.get_barrier_semaphore()
    partners = [up, down, lo, far, core] + group
    for partner in partners:
        pl.semaphore_signal(barrier, inc=1, device_id=partner, device_id_type=MESH)

    @pl.when(moves)
    def _():
        pl.semaphore_signal(barrier, inc=1, device_id=(from_r, from_c), device_id_type=MESH)

    def at(zz, l):
        return panel.at[rows((zz * 4 + l * 2 + k) * 64, 64)]

    def early(ref):
        return ref.at[:, pl.ds(0, EARLY)]

    def late(ref):
        return ref.at[:, pl.ds(EARLY, S - EARLY)]

    def half(ref, h):
        return ref.at[pl.ds(h * 32, 32)]

    panel[rows(c * 64, 64)] = own_ref[...]
    pl.semaphore_wait(barrier, len(partners) + jnp.where(moves, 1, 0))

    own = at(z, yl)
    E_OWN, UP, DOWN, UP_E, DOWN_E, LO, CORE, CORE_LO, COL = 0, 48, 56, 8, 12, 16, 24, 32, 40
    PERM = 47
    cp.start(E_OWN, early(own), early(own), lo)
    for h in (0, 1):
        cp.start(UP + h, half(own, h), half(own, h), up)
        cp.start(DOWN + h, half(own, h), half(own, h), down)
    permuted = copy(own, block.at[rows(to_r * 64, 64)], send.at[1], recv.at[PERM], (to_r, to_c))
    pl.when(moves)(permuted.start)

    @pl.when(jnp.logical_not(moves))
    def _():
        block[rows(r * 64, 64)] = own_ref[...]

    cp.start(LO, late(own), late(own), lo)
    cp.start(CORE, own, own, core)
    cp.make(E_OWN, early(own), early(own), lo).wait_recv()
    e = early(at(z, 1 - yl))
    cp.start(UP_E, e, e, up)
    cp.start(DOWN_E, e, e, down)

    def lo_arrived(i, zz):
        piece = at(zz, 1 - yl)
        cp.make(LO + i, late(piece), late(piece), lo).wait_recv()
        cp.start(CORE_LO + i, piece, piece, core)

    def relay(slot, ref, to, more):
        for h in (0, 1):
            part = half(ref, h)
            cp.make(slot + h, part, part, to).wait_recv()
            if more:
                cp.start(slot + 2 + h, part, part, to)

    def multiply(i, zz):
        cp.make(CORE + i, own, own, core).wait_recv()
        cp.make(CORE_LO + i, own, own, core).wait_recv()
        partial(zz)

    for t in range(1, 5):
        a = at((z + 8 - t) % 8, yl)
        b = at((z + t) % 8, yl)
        relay(UP + 2 * t - 2, a, up, t < 4)
        if t < 4:
            relay(DOWN + 2 * t - 2, b, down, t < 3)
        ea = early(at((z + 8 - t) % 8, 1 - yl))
        eb = early(at((z + t) % 8, 1 - yl))
        if t < 4:
            cp.make(UP_E + t - 1, ea, ea, up).wait_recv()
            if t < 3:
                cp.start(UP_E + t, ea, ea, up)
        cp.make(DOWN_E + t - 1, eb, eb, down).wait_recv()
        if t < 4:
            cp.start(DOWN_E + t, eb, eb, down)
        cp.start(LO + 2 * t - 1, late(a), late(a), lo)
        cp.start(CORE + 2 * t - 1, a, a, core)
        if t < 4:
            cp.start(LO + 2 * t, late(b), late(b), lo)
            cp.start(CORE + 2 * t, b, b, core)
        if t == 2:
            @pl.when(moves)
            def _():
                cp.make(PERM, own, own, lo).wait_recv()

            column_start(cp, block, x, y, z, k, COL)
        if t == 3:
            column_middle(cp, block, x, y, z, k, COL)
        if t == 1:
            lo_arrived(0, z)
        else:
            lo_arrived(2 * t - 3, (z + 8 - (t - 1)) % 8)
            lo_arrived(2 * t - 2, (z + t - 1) % 8)
        if t == 2:
            multiply(0, z)
        if t > 2:
            multiply(2 * t - 5, (z + 8 - (t - 2)) % 8)
            multiply(2 * t - 4, (z + t - 2) % 8)
    lo_arrived(7, (z + 4) % 8)
    multiply(5, (z + 5) % 8)
    multiply(6, (z + 3) % 8)
    multiply(7, (z + 4) % 8)
    for i in range(1, 7):
        cp.make(COL + i, own, own, core).wait_recv()

    def finish():
        sent = measure.at[pl.ds(0, 38 * 64)]
        cp.make(0, sent, sent, core).wait_send()
        pl.when(moves)(permuted.wait_send)

    return finish


def timetable(hops, near_is_mine):
    base = {"near": HOP * hops, "other": HOP * (4 - hops)}
    mine = base["near" if near_is_mine else "other"]
    events = [(LATE - 0.1, 0, "late sum", 0), (LATE + 2.0, 7, "column start", 0), (LATE + 5.0, 7, "column middle", 0)]
    for q in range(CHUNKS):
        for n, stream in enumerate(("near", "other")):
            events.append((base[stream] + q, 1 + n, stream + " early", q))
            events.append((LATE + base[stream] + q, 1 + n, stream + " whole", q))
        events.append((mine + q + HOP, 4, "far early", q))
        events.append((LATE + mine + q + HOP, 3, "far whole", q))
        events.append((LATE + mine + q + HOP + 0.1, 5, "lo", q))
        events.append((LATE + mine + q + 2 * HOP, 6, "lo far", q))
    return [(name, q) for _, _, name, q in sorted(events)]


RS, CORE, COL, Z, FAR, LO, LOF = 0, 1, 2, 9, 9 + 4 * CHUNKS, 9 + 6 * CHUNKS, 9 + 7 * CHUNKS
FED = 9 + 8 * CHUNKS
FEED, RS_EARLY = FED + 4, FED + 8
RECVS = FED + 9
S_RS, S_CORE, S_COL, S_NEAR, S_SOURCE, S_OTHER, S_FAR, S_LO, S_FED = 0, 1, 2, 3, 5, 7, 9, 11, 12
SENDS = 13


def gather_projected(acc, part, block, panel, inbox, fed, send, recv, where, meanwhile):
    x, y, z, k = where
    yl, yh = y % 2, y // 2
    r = yh * 4 + x
    up = device(x, y, (z + 1) % 8, k)
    down = device(x, y, (z + 7) % 8, k)
    lo = device(x, yh * 2 + 1 - yl, z, k)
    far = device(x, 3 - y, z, k)
    core = device(x, y, z, 1 - k)

    def early(ref):
        return ref.at[:, pl.ds(0, EARLY)]

    def late(ref):
        return ref.at[:, pl.ds(EARLY, S - EARLY)]

    def scatter(cut, slot):
        for i in range(1, 8):
            p = (r + i) % 8
            copy(cut(part.at[rows(p * 64, 64)]), cut(inbox.at[pl.ds((7 - i) * 64, 64)]), send.at[S_RS], recv.at[slot],
                 device(p % 4, p // 4 * 2 + yl, z, k)).start()

    part[:, :EARLY] = acc[:EARLY, :].T
    scatter(early, RS_EARLY)
    part[:, EARLY:] = acc[EARLY:, :].T
    scatter(late, RS)
    meanwhile()
    own_rows = rows(r * 64, 64)
    piece = column_piece(block, x, y, 0)
    column = Copies(send.at[S_COL], recv)
    copy(early(inbox), early(inbox), send.at[S_RS], recv.at[RS_EARLY], core).wait_recv()
    total = part[own_rows, :EARLY]
    for i in range(7):
        total = total + inbox[i * 64:(i + 1) * 64, :EARLY]
    block[own_rows, :EARLY] = total
    xs = z % 4
    feed = copy(early(piece), early(piece), send.at[S_COL], recv.at[FEED + x], device(xs, y, z, k))
    pl.when(x != xs)(feed.start)
    copy(early(piece), fed.at[rows(x * 64, 64)], send.at[S_FED], recv.at[FED + x], device(xs, (y + 2) % 4, z, k)).start()

    def late_sum():
        copy(late(inbox), late(inbox), send.at[S_RS], recv.at[RS], core).wait_recv()
        total = part[own_rows, EARLY:]
        for i in range(7):
            total = total + inbox[i * 64:(i + 1) * 64, EARLY:]
        block[own_rows, EARLY:] = total
        to_source = copy(late(piece), late(piece), send.at[S_COL], recv.at[COL + (xs + 4 - x) % 4], device(xs, y, z, k))
        pl.when(x != xs)(to_source.start)

    def column_arrival(i):
        column.make(COL + i, piece, piece, core).wait_recv()

    def fed_arrival(d):
        at = (x + 4 - d) % 4
        ref = fed.at[rows(at * 64, 64)]
        copy(ref, ref, send.at[S_FED], recv.at[FED + at], core).wait_recv()
        if d:
            copy(ref, ref, send.at[S_FED], recv.at[FEED + at], core).wait_recv()

    def column_start():
        for d in AROUND:
            c = column.make(COL + d, piece, piece, device((x + d) % 4, y, z, k))
            pl.when((x + d) % 4 != xs)(c.start)
        column.start(COL, piece, piece, device(x, (y + 2) % 4, z, k))

    lane = (yl * 2 + k) * 512
    flane = ((1 - yl) * 2 + k) * 512
    fyh = 1 - yh
    around = [(x + 4 - d) % 4 * 64 for d in (0,) + AROUND]
    within = {"own": [yh * 256 + a for a in around], "far": [fyh * 256 + a for a in around]}

    def chunk(base, half, q):
        return pl.ds(pl.multiple_of(base + within[half][q], CHUNK), CHUNK)

    def whole(base, half, q):
        return panel.at[chunk(base, half, q)]

    d0 = (z + 8 - x) % 8
    near = jnp.where(jnp.logical_or(d0 <= 2, d0 >= 6), 0, 1)
    d = (d0 + 4 * near) % 8
    rising = d <= 2
    on = tuple(jnp.where(rising, a, b) for a, b in zip(up, down))
    back = tuple(jnp.where(rising, b, a) for a, b in zip(up, down))
    hops = jnp.where(rising, d, 8 - d)
    near_is_mine = near == yh

    def run(h, near_mine):
        def relay(stream, kind, q):
            n = 0 if kind == "whole" else 1
            mine = (stream == "near") == near_mine
            base = lane if mine else 2048
            cut, halves = (early, ("own", "far")) if n else (late, ("own",))
            refs = [cut(whole(base, half, q)) for half in halves]
            slot = recv.at[Z + ((0 if mine else 1) * CHUNKS + q) * 2 + n]
            source = stream == "near" and h == 0
            if source:
                dist = ((0,) + AROUND)[q]
                if n:
                    fed_arrival(dist)
                    panel[chunk(base, "own", q), :EARLY] = block[chunk(0, "own", q), :EARLY]
                    panel[chunk(base, "far", q), :EARLY] = fed[rows(around[q], 64)]
                else:
                    if q:
                        copy(late(piece), late(piece), send.at[S_COL], recv.at[COL + dist], core).wait_recv()
                    panel[chunk(base, "own", q), EARLY:] = block[chunk(0, "own", q), EARLY:]
            else:
                both = panel.at[pl.ds(0, 128), pl.ds(0, EARLY)] if n else refs[0]
                copy(both, both, send.at[S_NEAR], slot, core).wait_recv()
            for ref, half in zip(refs, halves):
                if source:
                    copy(ref, ref, send.at[S_SOURCE + n], slot, down).start()
                if stream == "near":
                    copy(ref, ref, send.at[S_NEAR + n], slot, on).start()
                elif h > 0:
                    c = copy(ref, ref, send.at[S_OTHER + n], slot, back)
                    if h == 2:
                        c.start()
                    else:
                        pl.when(rising if n else jnp.logical_not(rising))(c.start)
                if not mine:
                    copy(ref, cut(whole(lane, half, q)), send.at[S_FAR + n], recv.at[FAR + 2 * q + n], far).start()
            if mine and not n:
                copy(refs[0], refs[0], send.at[S_LO], recv.at[LO + q], lo).start()
                to_core(whole(lane, "own", q))

        def arrive(ref, slot):
            copy(ref, ref, send.at[S_CORE], recv.at[slot], core).wait_recv()

        def to_core(ref):
            copy(ref, ref, send.at[S_CORE], recv.at[CORE], core).start()

        for name, q in timetable(h, near_mine):
            if name == "late sum":
                late_sum()
            elif name == "column start":
                column_start()
            elif name == "column middle":
                column_middle(column, block, x, y, z, k, COL)
            elif name == "far whole":
                ref = whole(flane, "far", q)
                arrive(late(ref), FAR + 2 * q)
                copy(late(ref), late(ref), send.at[S_LO], recv.at[LOF + q], lo).start()
                to_core(ref)
            elif name == "far early":
                arrive(panel.at[pl.ds(0, 128), pl.ds(0, EARLY)], FAR + 2 * q + 1)
            elif name == "lo":
                ref = whole(flane, "own", q)
                arrive(late(ref), LO + q)
                to_core(ref)
            elif name == "lo far":
                ref = whole(lane, "far", q)
                arrive(late(ref), LOF + q)
                to_core(ref)
            else:
                relay(*name.split(), q)
        for i in range(1 if h else 4, 7):
            column_arrival(i)

    for h in (0, 1, 2):
        for near_mine in (True, False):
            pl.when(jnp.logical_and(hops == h, near_is_mine if near_mine else jnp.logical_not(near_is_mine)))(
                lambda h=h, near_mine=near_mine: run(h, near_mine))

    def sized(n, columns=S):
        return panel.at[pl.ds(0, n), pl.ds(0, columns)]

    got = sized(1024)
    copy(got, got, send.at[S_CORE], recv.at[CORE], core).wait_recv()

    def finish():
        def sent(slot, ref, cond=None):
            c = copy(ref, ref, send.at[slot], recv.at[RS], core)
            if cond is None:
                c.wait_send()
            else:
                pl.when(cond)(c.wait_send)

        sent(S_RS, sized(448))
        sent(S_COL, sized(448))
        sent(S_CORE, got)
        sent(S_LO, sized(512, S - EARLY))
        sent(S_FED, sized(64, EARLY))
        for n, ref in enumerate((sized(256, S - EARLY), sized(512, EARLY))):
            sent(S_NEAR + n, ref)
            sent(S_FAR + n, ref)
            sent(S_SOURCE + n, ref, hops == 0)
            sent(S_OTHER + n, ref, jnp.logical_or(hops == 2, jnp.logical_and(
                hops == 1, rising if n else jnp.logical_not(rising))))

    return finish


TILE = 512


def update_tile(i, where, count, samples, projected, omega, left, right):
    x, y, z, k = where
    at = rows(i * TILE, TILE)
    for j, ref in enumerate((samples, projected)):
        hi, lo = split(ref[at])
        left[:, j * S:(j + 1) * S] = hi
        left[:, (j + 2) * S:(j + 3) * S] = hi
        left[:, (j + 4) * S:(j + 5) * S] = lo
    cross = lax.dot_general(left[...], right[...], (((1,), (1,)), ((), ())), preferred_element_type=F32)
    old = omega[at]
    moved = old - (STEP * 0.5 / count) * cross
    threshold = STEP * PENALTY
    new = moved - jnp.clip(moved, -threshold, threshold)
    omega[at] = new

    @pl.when(((y // 2) * 4 + x) * 4 + i == z * 4 + (y % 2) * 2 + k)
    def _():
        shape = (TILE, TILE)
        on = lax.broadcasted_iota(jnp.int32, shape, 0) == lax.broadcasted_iota(jnp.int32, shape, 1)
        safe = jnp.where(on, old, 1.0)
        omega[at] = jnp.where(on, moved + STEP / safe, new)


def set_right(right, block, first):
    hi, lo = split(block[...])
    right[:, first * S:(first + 1) * S] = hi
    right[:, (first + 2) * S:(first + 3) * S] = lo
    right[:, (first + 4) * S:(first + 5) * S] = hi


def kernel(own_ref, omega_ref, omega, samples, samples_block, flipped, acc, part, part1, projected0, projected1,
           block0, block1, inbox0, inbox1, fed0, fed1, left, right, tall, x_send, x_recv, send0, recv0, send1, recv1, in_sem):
    where = place()
    load = pltpu.make_async_copy(omega_ref, omega, in_sem)
    load.start()
    acc[...] = jnp.zeros_like(acc)
    loaded = []

    def partial(zz):
        flip_block(zz, flipped, samples)
        if not loaded:
            load.wait()
            loaded.append(True)
        partial_block(zz, acc, flipped, omega, tall)

    finish = gather_samples(own_ref, samples, samples_block, projected0, x_send, x_recv, where, partial)
    finish = gather_projected(acc, part, block0, projected0, inbox0, fed0, send0, recv0, where, finish)
    set_right(right, samples_block, 1)
    set_right(right, block0, 0)
    acc[...] = jnp.zeros_like(acc)

    def first(i, _):
        update_tile(i, where, S, samples, projected0, omega, left, right)
        partial_block(2 * i, acc, flipped, omega, tall)
        partial_block(2 * i + 1, acc, flipped, omega, tall)
        return 0

    lax.fori_loop(0, 2048 // TILE, first, 0)
    finish = gather_projected(acc, part1, block1, projected1, inbox1, fed1, send1, recv1, where, finish)
    set_right(right, block1, 0)

    def second(i, _):
        update_tile(i, where, S, samples, projected1, omega, left, right)
        return 0

    lax.fori_loop(0, 2048 // TILE, second, 0)
    finish()


def body(samples, omega):
    dma = pltpu.SemaphoreType.DMA
    vmem = pltpu.VMEM
    return pl.pallas_call(
        kernel,
        out_shape=pltpu.VMEM((2048, 512), F32),
        in_specs=[pl.BlockSpec(memory_space=pltpu.VMEM), pl.BlockSpec(memory_space=pltpu.HBM)],
        out_specs=pl.BlockSpec(memory_space=pltpu.VMEM),
        scratch_shapes=[
            vmem((2048, S), F32), vmem((512, S), F32), vmem((8, S, 3 * BLOCK), BF16),
            vmem((S, 512), F32), vmem((512, S), F32), vmem((512, S), F32), vmem((2560, S), F32), vmem((2560, S), F32),
            vmem((512, S), F32), vmem((512, S), F32), vmem((7 * 64, S), F32), vmem((7 * 64, S), F32), vmem((256, EARLY), F32), vmem((256, EARLY), F32),
            vmem((TILE, K3), BF16), vmem((512, K3), BF16), vmem((3 * BLOCK, 512), BF16),
            dma((2,)), dma((62,)), dma((SENDS,)), dma((RECVS,)), dma((SENDS,)), dma((RECVS,)), dma,
        ],
        compiler_params=pltpu.CompilerParams(collective_id=0, has_side_effects=True, vmem_limit_bytes=VMEM_LIMIT),
        name="concord_steps",
    )(samples.T, omega)


def solution(mesh):
    in_specs = (P(None, ("row", "col")), P("row", "col"))
    out_specs = P("row", "col")
    return jax.shard_map(body, mesh=mesh, in_specs=in_specs, out_specs=out_specs, check_vma=False)
```

```python
import jax
import jax.numpy as jnp
from jax import lax
from jax.experimental import pallas as pl
from jax.experimental.pallas import tpu as pltpu
from jax.sharding import PartitionSpec as P

ITERS = 2
STEP = 0.01
PENALTY = 0.25
S = 384
EARLY = 128
MESH = pl.DeviceIdType.MESH
F32 = jnp.float32
BF16 = jnp.bfloat16
VMEM_LIMIT = 58 * 2**20


def place():
    r = lax.axis_index("row")
    c = lax.axis_index("col")
    return r % 4, (r // 4) * 2 + (c // 2) % 2, c // 4, c % 2


def device(x, y, z, k):
    return (y // 2) * 4 + x, z * 4 + (y % 2) * 2 + k


def rows(start, size):
    return pl.ds(pl.multiple_of(start, 64), size)


def copy(src, dst, send, recv, to):
    return pltpu.make_async_remote_copy(
        src_ref=src, dst_ref=dst, send_sem=send, recv_sem=recv, device_id=to, device_id_type=MESH)


class Copies:
    def __init__(self, send, recv):
        self.send, self.recv = send, recv

    def make(self, slot, src, dst, to):
        return copy(src, dst, self.send, self.recv.at[slot], to)

    def start(self, slot, src, dst, to):
        self.make(slot, src, dst, to).start()


def column_piece(buf, x, y, d, e=0):
    return buf.at[rows((((y + e) % 4) // 2 * 4 + (x + 4 - d) % 4) * 64, 64)]


AROUND = (1, 3, 2)


def column_start(cp, buf, x, y, z, k, base):
    mine = column_piece(buf, x, y, 0)
    for d in AROUND:
        cp.start(base + d, mine, mine, device((x + d) % 4, y, z, k))
    cp.start(base, mine, mine, device(x, (y + 2) % 4, z, k))


def column_middle(cp, buf, x, y, z, k, base):
    theirs = column_piece(buf, x, y, 0, 2)
    cp.make(base, theirs, theirs, (0, 0)).wait_recv()
    for d in AROUND:
        cp.start(base + 3 + d, theirs, theirs, device((x + d) % 4, y, z, k))


CHUNK = 64
CHUNKS = 4
HOP = 2.1
LATE = 4.0
K3 = 6 * S
BLOCK = 256


def split(a):
    hi = a.astype(BF16)
    return hi, (a - hi.astype(F32)).astype(BF16)


def partial_block(i, acc, flipped, omega, right):
    hi, lo = split(omega[rows(i * BLOCK, BLOCK)])
    right[:BLOCK] = hi
    right[BLOCK:2 * BLOCK] = lo
    right[2 * BLOCK:] = hi
    acc[...] += jnp.dot(flipped[i], right[...], preferred_element_type=F32)


def flip_block(i, flipped, panel):
    hi, lo = split(panel[rows(i * BLOCK, BLOCK)].T)
    flipped[i, :, :BLOCK] = hi
    flipped[i, :, BLOCK:2 * BLOCK] = hi
    flipped[i, :, 2 * BLOCK:] = lo


def gather_samples(own_ref, panel, block, measure, send, recv, where, partial):
    x, y, z, k = where
    yl, yh = y % 2, y // 2
    r, c = yh * 4 + x, z * 4 + yl * 2 + k
    up = device(x, y, (z + 1) % 8, k)
    down = device(x, y, (z + 7) % 8, k)
    lo = device(x, yh * 2 + 1 - yl, z, k)
    far = device(x, 3 - y, z, k)
    core = device(x, y, z, 1 - k)
    to_r, to_c = c % 8, r * 4 + c // 8
    own_b = c * 8 + r
    from_r, from_c = own_b // 32, own_b % 32
    moves = (to_r * 32 + to_c) != (r * 32 + c)
    group = [device((x + d) % 4, (y + e) % 4, z, k) for d in range(4) for e in (0, 2) if d or e]
    cp = Copies(send.at[0], recv)

    barrier = pltpu.get_barrier_semaphore()
    partners = [up, down, lo, far, core] + group
    for partner in partners:
        pl.semaphore_signal(barrier, inc=1, device_id=partner, device_id_type=MESH)

    @pl.when(moves)
    def _():
        pl.semaphore_signal(barrier, inc=1, device_id=(from_r, from_c), device_id_type=MESH)

    def at(zz, l):
        return panel.at[rows((zz * 4 + l * 2 + k) * 64, 64)]

    def early(ref):
        return ref.at[:, pl.ds(0, EARLY)]

    def late(ref):
        return ref.at[:, pl.ds(EARLY, S - EARLY)]

    def half(ref, h):
        return ref.at[pl.ds(h * 32, 32)]

    panel[rows(c * 64, 64)] = own_ref[...]
    pl.semaphore_wait(barrier, len(partners) + jnp.where(moves, 1, 0))

    own = at(z, yl)
    E_OWN, UP, DOWN, UP_E, DOWN_E, LO, CORE, CORE_LO, COL = 0, 48, 56, 8, 12, 16, 24, 32, 40
    PERM = 47
    cp.start(E_OWN, early(own), early(own), lo)
    for h in (0, 1):
        cp.start(UP + h, half(own, h), half(own, h), up)
        cp.start(DOWN + h, half(own, h), half(own, h), down)
    permuted = copy(own, block.at[rows(to_r * 64, 64)], send.at[1], recv.at[PERM], (to_r, to_c))
    pl.when(moves)(permuted.start)

    @pl.when(jnp.logical_not(moves))
    def _():
        block[rows(r * 64, 64)] = own_ref[...]

    cp.start(LO, late(own), late(own), lo)
    cp.start(CORE, own, own, core)
    cp.make(E_OWN, early(own), early(own), lo).wait_recv()
    e = early(at(z, 1 - yl))
    cp.start(UP_E, e, e, up)
    cp.start(DOWN_E, e, e, down)

    def lo_arrived(i, zz):
        piece = at(zz, 1 - yl)
        cp.make(LO + i, late(piece), late(piece), lo).wait_recv()
        cp.start(CORE_LO + i, piece, piece, core)

    def relay(slot, ref, to, more):
        for h in (0, 1):
            part = half(ref, h)
            cp.make(slot + h, part, part, to).wait_recv()
            if more:
                cp.start(slot + 2 + h, part, part, to)

    def multiply(i, zz):
        cp.make(CORE + i, own, own, core).wait_recv()
        cp.make(CORE_LO + i, own, own, core).wait_recv()
        partial(zz)

    for t in range(1, 5):
        a = at((z + 8 - t) % 8, yl)
        b = at((z + t) % 8, yl)
        relay(UP + 2 * t - 2, a, up, t < 4)
        if t < 4:
            relay(DOWN + 2 * t - 2, b, down, t < 3)
        ea = early(at((z + 8 - t) % 8, 1 - yl))
        eb = early(at((z + t) % 8, 1 - yl))
        if t < 4:
            cp.make(UP_E + t - 1, ea, ea, up).wait_recv()
            if t < 3:
                cp.start(UP_E + t, ea, ea, up)
        cp.make(DOWN_E + t - 1, eb, eb, down).wait_recv()
        if t < 4:
            cp.start(DOWN_E + t, eb, eb, down)
        cp.start(LO + 2 * t - 1, late(a), late(a), lo)
        cp.start(CORE + 2 * t - 1, a, a, core)
        if t < 4:
            cp.start(LO + 2 * t, late(b), late(b), lo)
            cp.start(CORE + 2 * t, b, b, core)
        if t == 2:
            @pl.when(moves)
            def _():
                cp.make(PERM, own, own, lo).wait_recv()

            column_start(cp, block, x, y, z, k, COL)
        if t == 3:
            column_middle(cp, block, x, y, z, k, COL)
        if t == 1:
            lo_arrived(0, z)
        else:
            lo_arrived(2 * t - 3, (z + 8 - (t - 1)) % 8)
            lo_arrived(2 * t - 2, (z + t - 1) % 8)
        if t == 2:
            multiply(0, z)
        if t > 2:
            multiply(2 * t - 5, (z + 8 - (t - 2)) % 8)
            multiply(2 * t - 4, (z + t - 2) % 8)
    lo_arrived(7, (z + 4) % 8)
    multiply(5, (z + 5) % 8)
    multiply(6, (z + 3) % 8)
    multiply(7, (z + 4) % 8)
    for i in range(1, 7):
        cp.make(COL + i, own, own, core).wait_recv()

    def finish():
        sent = measure.at[pl.ds(0, 38 * 64)]
        cp.make(0, sent, sent, core).wait_send()
        pl.when(moves)(permuted.wait_send)

    return finish


def timetable(hops, near_is_mine):
    base = {"near": HOP * hops, "other": HOP * (4 - hops)}
    mine = base["near" if near_is_mine else "other"]
    events = [(LATE - 0.1, 0, "late sum", 0), (LATE + 2.0, 7, "column start", 0), (LATE + 5.0, 7, "column middle", 0)]
    for q in range(CHUNKS):
        for n, stream in enumerate(("near", "other")):
            events.append((base[stream] + q, 1 + n, stream + " early", q))
            events.append((LATE + base[stream] + q, 1 + n, stream + " whole", q))
        events.append((mine + q + HOP, 4, "far early", q))
        events.append((LATE + mine + q + HOP, 3, "far whole", q))
        events.append((LATE + mine + q + HOP + 0.1, 5, "lo", q))
        events.append((LATE + mine + q + 2 * HOP, 6, "lo far", q))
    return [(name, q) for _, _, name, q in sorted(events)]


RS, CORE, COL, Z, FAR, LO, LOF = 0, 1, 2, 9, 9 + 4 * CHUNKS, 9 + 6 * CHUNKS, 9 + 7 * CHUNKS
FED = 9 + 8 * CHUNKS
FEED, RS_EARLY = FED + 4, FED + 8
RECVS = FED + 9
S_RS, S_CORE, S_COL, S_NEAR, S_SOURCE, S_OTHER, S_FAR, S_LO, S_FED = 0, 1, 2, 3, 5, 7, 9, 11, 12
SENDS = 13


def gather_projected(acc, part, block, panel, inbox, fed, send, recv, where, meanwhile):
    x, y, z, k = where
    yl, yh = y % 2, y // 2
    r = yh * 4 + x
    up = device(x, y, (z + 1) % 8, k)
    down = device(x, y, (z + 7) % 8, k)
    lo = device(x, yh * 2 + 1 - yl, z, k)
    far = device(x, 3 - y, z, k)
    core = device(x, y, z, 1 - k)

    def early(ref):
        return ref.at[:, pl.ds(0, EARLY)]

    def late(ref):
        return ref.at[:, pl.ds(EARLY, S - EARLY)]

    def scatter(cut, slot):
        for i in range(1, 8):
            p = (r + i) % 8
            copy(cut(part.at[rows(p * 64, 64)]), cut(inbox.at[pl.ds((7 - i) * 64, 64)]), send.at[S_RS], recv.at[slot],
                 device(p % 4, p // 4 * 2 + yl, z, k)).start()

    part[:, :EARLY] = acc[:EARLY, :].T
    scatter(early, RS_EARLY)
    part[:, EARLY:] = acc[EARLY:, :].T
    scatter(late, RS)
    meanwhile()
    own_rows = rows(r * 64, 64)
    piece = column_piece(block, x, y, 0)
    column = Copies(send.at[S_COL], recv)
    copy(early(inbox), early(inbox), send.at[S_RS], recv.at[RS_EARLY], core).wait_recv()
    total = part[own_rows, :EARLY]
    for i in range(7):
        total = total + inbox[i * 64:(i + 1) * 64, :EARLY]
    block[own_rows, :EARLY] = total
    xs = z % 4
    feed = copy(early(piece), early(piece), send.at[S_COL], recv.at[FEED + x], device(xs, y, z, k))
    pl.when(x != xs)(feed.start)
    copy(early(piece), fed.at[rows(x * 64, 64)], send.at[S_FED], recv.at[FED + x], device(xs, (y + 2) % 4, z, k)).start()

    def late_sum():
        copy(late(inbox), late(inbox), send.at[S_RS], recv.at[RS], core).wait_recv()
        total = part[own_rows, EARLY:]
        for i in range(7):
            total = total + inbox[i * 64:(i + 1) * 64, EARLY:]
        block[own_rows, EARLY:] = total
        to_source = copy(late(piece), late(piece), send.at[S_COL], recv.at[COL + (xs + 4 - x) % 4], device(xs, y, z, k))
        pl.when(x != xs)(to_source.start)

    def column_arrival(i):
        column.make(COL + i, piece, piece, core).wait_recv()

    def fed_arrival(d):
        at = (x + 4 - d) % 4
        ref = fed.at[rows(at * 64, 64)]
        copy(ref, ref, send.at[S_FED], recv.at[FED + at], core).wait_recv()
        if d:
            copy(ref, ref, send.at[S_FED], recv.at[FEED + at], core).wait_recv()

    def column_start():
        for d in AROUND:
            c = column.make(COL + d, piece, piece, device((x + d) % 4, y, z, k))
            pl.when((x + d) % 4 != xs)(c.start)
        column.start(COL, piece, piece, device(x, (y + 2) % 4, z, k))

    lane = (yl * 2 + k) * 512
    flane = ((1 - yl) * 2 + k) * 512
    fyh = 1 - yh
    around = [(x + 4 - d) % 4 * 64 for d in (0,) + AROUND]
    within = {"own": [yh * 256 + a for a in around], "far": [fyh * 256 + a for a in around]}

    def chunk(base, half, q):
        return pl.ds(pl.multiple_of(base + within[half][q], CHUNK), CHUNK)

    def whole(base, half, q):
        return panel.at[chunk(base, half, q)]

    d0 = (z + 8 - x) % 8
    near = jnp.where(jnp.logical_or(d0 <= 2, d0 >= 6), 0, 1)
    d = (d0 + 4 * near) % 8
    rising = d <= 2
    on = tuple(jnp.where(rising, a, b) for a, b in zip(up, down))
    back = tuple(jnp.where(rising, b, a) for a, b in zip(up, down))
    hops = jnp.where(rising, d, 8 - d)
    near_is_mine = near == yh

    def run(h, near_mine):
        def relay(stream, kind, q):
            n = 0 if kind == "whole" else 1
            mine = (stream == "near") == near_mine
            base = lane if mine else 2048
            cut, halves = (early, ("own", "far")) if n else (late, ("own",))
            refs = [cut(whole(base, half, q)) for half in halves]
            slot = recv.at[Z + ((0 if mine else 1) * CHUNKS + q) * 2 + n]
            source = stream == "near" and h == 0
            if source:
                dist = ((0,) + AROUND)[q]
                if n:
                    fed_arrival(dist)
                    panel[chunk(base, "own", q), :EARLY] = block[chunk(0, "own", q), :EARLY]
                    panel[chunk(base, "far", q), :EARLY] = fed[rows(around[q], 64)]
                else:
                    if q:
                        copy(late(piece), late(piece), send.at[S_COL], recv.at[COL + dist], core).wait_recv()
                    panel[chunk(base, "own", q), EARLY:] = block[chunk(0, "own", q), EARLY:]
            else:
                both = panel.at[pl.ds(0, 128), pl.ds(0, EARLY)] if n else refs[0]
                copy(both, both, send.at[S_NEAR], slot, core).wait_recv()
            for ref, half in zip(refs, halves):
                if source:
                    copy(ref, ref, send.at[S_SOURCE + n], slot, down).start()
                if stream == "near":
                    copy(ref, ref, send.at[S_NEAR + n], slot, on).start()
                elif h > 0:
                    c = copy(ref, ref, send.at[S_OTHER + n], slot, back)
                    if h == 2:
                        c.start()
                    else:
                        pl.when(rising if n else jnp.logical_not(rising))(c.start)
                if not mine:
                    copy(ref, cut(whole(lane, half, q)), send.at[S_FAR + n], recv.at[FAR + 2 * q + n], far).start()
            if mine and not n:
                copy(refs[0], refs[0], send.at[S_LO], recv.at[LO + q], lo).start()
                to_core(whole(lane, "own", q))

        def arrive(ref, slot):
            copy(ref, ref, send.at[S_CORE], recv.at[slot], core).wait_recv()

        def to_core(ref):
            copy(ref, ref, send.at[S_CORE], recv.at[CORE], core).start()

        for name, q in timetable(h, near_mine):
            if name == "late sum":
                late_sum()
            elif name == "column start":
                column_start()
            elif name == "column middle":
                column_middle(column, block, x, y, z, k, COL)
            elif name == "far whole":
                ref = whole(flane, "far", q)
                arrive(late(ref), FAR + 2 * q)
                copy(late(ref), late(ref), send.at[S_LO], recv.at[LOF + q], lo).start()
                to_core(ref)
            elif name == "far early":
                arrive(panel.at[pl.ds(0, 128), pl.ds(0, EARLY)], FAR + 2 * q + 1)
            elif name == "lo":
                ref = whole(flane, "own", q)
                arrive(late(ref), LO + q)
                to_core(ref)
            elif name == "lo far":
                ref = whole(lane, "far", q)
                arrive(late(ref), LOF + q)
                to_core(ref)
            else:
                relay(*name.split(), q)
        for i in range(1 if h else 4, 7):
            column_arrival(i)

    for h in (0, 1, 2):
        for near_mine in (True, False):
            pl.when(jnp.logical_and(hops == h, near_is_mine if near_mine else jnp.logical_not(near_is_mine)))(
                lambda h=h, near_mine=near_mine: run(h, near_mine))

    def sized(n, columns=S):
        return panel.at[pl.ds(0, n), pl.ds(0, columns)]

    got = sized(1024)
    copy(got, got, send.at[S_CORE], recv.at[CORE], core).wait_recv()

    def finish():
        def sent(slot, ref, cond=None):
            c = copy(ref, ref, send.at[slot], recv.at[RS], core)
            if cond is None:
                c.wait_send()
            else:
                pl.when(cond)(c.wait_send)

        sent(S_RS, sized(448))
        sent(S_COL, sized(448))
        sent(S_CORE, got)
        sent(S_LO, sized(512, S - EARLY))
        sent(S_FED, sized(64, EARLY))
        for n, ref in enumerate((sized(256, S - EARLY), sized(512, EARLY))):
            sent(S_NEAR + n, ref)
            sent(S_FAR + n, ref)
            sent(S_SOURCE + n, ref, hops == 0)
            sent(S_OTHER + n, ref, jnp.logical_or(hops == 2, jnp.logical_and(
                hops == 1, rising if n else jnp.logical_not(rising))))

    return finish


TILE = 512


def set_left(i, ref, left, j):
    hi, lo = split(ref[rows(i * TILE, TILE)])
    left[i, :, j * S:(j + 1) * S] = hi
    left[i, :, (j + 2) * S:(j + 3) * S] = hi
    left[i, :, (j + 4) * S:(j + 5) * S] = lo


def update_tile(i, where, count, projected, omega, left, right):
    x, y, z, k = where
    at = rows(i * TILE, TILE)
    set_left(i, projected, left, 1)
    cross = lax.dot_general(left[i], right[...], (((1,), (1,)), ((), ())), preferred_element_type=F32)
    old = omega[at]
    moved = old - (STEP * 0.5 / count) * cross
    threshold = STEP * PENALTY
    new = moved - jnp.clip(moved, -threshold, threshold)
    omega[at] = new

    @pl.when(((y // 2) * 4 + x) * 4 + i == z * 4 + (y % 2) * 2 + k)
    def _():
        shape = (TILE, TILE)
        on = lax.broadcasted_iota(jnp.int32, shape, 0) == lax.broadcasted_iota(jnp.int32, shape, 1)
        safe = jnp.where(on, old, 1.0)
        omega[at] = jnp.where(on, moved + STEP / safe, new)


def set_right(right, block, first):
    hi, lo = split(block[...])
    right[:, first * S:(first + 1) * S] = hi
    right[:, (first + 2) * S:(first + 3) * S] = lo
    right[:, (first + 4) * S:(first + 5) * S] = hi


def kernel(own_ref, omega_ref, omega, samples, samples_block, flipped, acc, part, part1, projected0, projected1,
           block0, block1, inbox0, inbox1, fed0, fed1, left, right, tall, x_send, x_recv, send0, recv0, send1, recv1, in_sem):
    where = place()
    load = pltpu.make_async_copy(omega_ref, omega, in_sem)
    load.start()
    acc[...] = jnp.zeros_like(acc)
    loaded = []

    def partial(zz):
        flip_block(zz, flipped, samples)
        if not loaded:
            load.wait()
            loaded.append(True)
        partial_block(zz, acc, flipped, omega, tall)

    finish = gather_samples(own_ref, samples, samples_block, projected0, x_send, x_recv, where, partial)
    samples_sent = finish

    def prepare():
        samples_sent()
        set_right(right, samples_block, 1)

        def tile(i, _):
            set_left(i, samples, left, 0)
            return 0

        lax.fori_loop(0, 2048 // TILE, tile, 0)

    finish = gather_projected(acc, part, block0, projected0, inbox0, fed0, send0, recv0, where, prepare)
    set_right(right, block0, 0)
    acc[...] = jnp.zeros_like(acc)

    def first(i, _):
        update_tile(i, where, S, projected0, omega, left, right)
        partial_block(2 * i, acc, flipped, omega, tall)
        partial_block(2 * i + 1, acc, flipped, omega, tall)
        return 0

    lax.fori_loop(0, 2048 // TILE, first, 0)
    finish = gather_projected(acc, part1, block1, projected1, inbox1, fed1, send1, recv1, where, finish)
    set_right(right, block1, 0)

    def second(i, _):
        update_tile(i, where, S, projected1, omega, left, right)
        return 0

    lax.fori_loop(0, 2048 // TILE, second, 0)
    finish()


def body(samples, omega):
    dma = pltpu.SemaphoreType.DMA
    vmem = pltpu.VMEM
    return pl.pallas_call(
        kernel,
        out_shape=pltpu.VMEM((2048, 512), F32),
        in_specs=[pl.BlockSpec(memory_space=pltpu.VMEM), pl.BlockSpec(memory_space=pltpu.HBM)],
        out_specs=pl.BlockSpec(memory_space=pltpu.VMEM),
        scratch_shapes=[
            vmem((2048, S), F32), vmem((512, S), F32), vmem((8, S, 3 * BLOCK), BF16),
            vmem((S, 512), F32), vmem((512, S), F32), vmem((512, S), F32), vmem((2560, S), F32), vmem((2560, S), F32),
            vmem((512, S), F32), vmem((512, S), F32), vmem((7 * 64, S), F32), vmem((7 * 64, S), F32), vmem((256, EARLY), F32), vmem((256, EARLY), F32),
            vmem((2048 // TILE, TILE, K3), BF16), vmem((512, K3), BF16), vmem((3 * BLOCK, 512), BF16),
            dma((2,)), dma((62,)), dma((SENDS,)), dma((RECVS,)), dma((SENDS,)), dma((RECVS,)), dma,
        ],
        compiler_params=pltpu.CompilerParams(collective_id=0, has_side_effects=True, vmem_limit_bytes=VMEM_LIMIT),
        name="concord_steps",
    )(samples.T, omega)


def solution(mesh):
    in_specs = (P(None, ("row", "col")), P("row", "col"))
    out_specs = P("row", "col")
    return jax.shard_map(body, mesh=mesh, in_specs=in_specs, out_specs=out_specs, check_vma=False)
```
